128 devices in a mesh: dp: 32 (over y, z, core), mp: 4 (over x).
Axes of the slice: x: 4, y: 4, z: 4, core: 2. Of those that a mesh axis runs over, the one named last changes fastest.
Arguments:
- candidates: bfloat16 [1024, 128, 1024], P('dp', None, 'mp'), may hold values from -24 to 24
- live_counts: int32 [1024], P('dp'), may hold values from 1 to 128
- request_user: int32 [1024], P('dp'), may hold values from 0 to 1023, as said below
- score_slot: int32 [1024], replicated, may hold values from 0 to 1023, as said below
- history_cache: bfloat16 [1024, 256, 2048], P('dp', None, 'mp'), may hold values from -6 to 6
- history_length: int32 [1024], P('dp'), may hold values from 1 to 256, as said below
- input_weight: bfloat16 [1024, 4096], P(None, 'mp'), may hold values from -0.1875 to 0.1875
- time_bias: float32 [8, 16], P('mp'), may hold values from -4 to 4
- output_weight: bfloat16 [1024, 1024], P('mp'), may hold values from -0.1875 to 0.1875
Outputs:
- updated: bfloat16 [1024, 128, 1024], P('dp', None, 'mp')
The draws below stay inside these ranges and needn't reach their ends.
Inputs may be any that keep to these rules, and one draw needn't show every extreme that they name: `request_user`: A permutation: each user has exactly one request. `score_slot`: A permutation. The scoring rank of user u is score_slot[u] // 32, so every rank scores exactly 32 users. At most 1 of the users of one dp index (users d * 32 to d * 32 + 31), and at most 1 of the requests held on one dp index, have the same scoring rank; both bounds are reached in every draw. `history_length`: some user has exactly 256 events.
All inputs are finite; a program needn't handle non-finite values.
Results may differ from the reference program's by a relative error of at most 0.0039.
Values may be sent and summed in bfloat16 or wider, within the bound.
No kernel may reach another device: no remote copies, remote signals or barrier semaphores. Data moves between devices by JAX's collectives and lax.ppermute only.
A program may use at most 128 MiB of HBM per device.

```python
import math
import jax
import jax.numpy as jnp
from jax import lax

D = 1024
H = 8
HD = 128
UD = 32
NCR = 128
NBKT = 16
HEV = 256
USERS = 1024
N_DP = 32


def half_first(order):
    half = order.shape[0] // 2
    where_half = jnp.argmax((order == half).astype(jnp.int32)).astype(jnp.int32)
    first = order[0]
    return order.at[where_half].set(first).at[0].set(half).astype(jnp.int32)


def shared_layout(key):
    key_shift, key_offset, key_owner, key_scorer, key_ingest = jax.random.split(key, 5)
    rank_ids = jnp.arange(N_DP, dtype=jnp.int32)
    classes = jnp.arange(UD, dtype=jnp.int32)
    shifts = half_first(jax.random.permutation(key_shift, N_DP).astype(jnp.int32))
    offsets = half_first(jax.random.permutation(key_offset, N_DP).astype(jnp.int32))

    def per_rank_orders(base_key):
        return jax.vmap(lambda number: jax.random.permutation(jax.random.fold_in(base_key, number), UD))(rank_ids).astype(jnp.int32)
    owner_order = per_rank_orders(key_owner)
    scorer_order = per_rank_orders(key_scorer)
    ingest_order = per_rank_orders(key_ingest)
    owner_inverse = jnp.argsort(owner_order, axis=1).astype(jnp.int32)
    scorer_grid = (rank_ids[:, None] + shifts[owner_order % N_DP]) % N_DP
    slot_grid = scorer_grid * UD + scorer_order[scorer_grid, owner_order]
    score_slot = slot_grid.reshape(USERS).astype(jnp.int32)
    wrapped = classes % N_DP
    scorer_of = (rank_ids[:, None] - offsets[wrapped][None, :]) % N_DP
    owner_of = (scorer_of - shifts[wrapped][None, :]) % N_DP
    local_of = owner_inverse[owner_of, jnp.broadcast_to(classes[None, :], owner_of.shape)]
    user_grid = owner_of * UD + local_of
    placed = jnp.zeros((N_DP, UD), jnp.int32).at[jnp.broadcast_to(rank_ids[:, None], ingest_order.shape), ingest_order].set(user_grid)
    return (score_slot, placed.reshape(USERS).astype(jnp.int32))


def draw_score_slot(key, part):
    return shared_layout(key)[0]


def draw_request_user(key, part):
    return shared_layout(key)[1]


def draw_history_length(key, part):
    key = jax.random.fold_in(key, 5)
    key_heavy, key_length, key_top = jax.random.split(key, 3)
    heavy = jax.random.randint(key_heavy, (N_DP, 1), 1, 5)
    ceiling = HEV * heavy // 4
    lengths = jax.random.randint(key_length, (N_DP, UD), 1, ceiling + 1).reshape(USERS)
    chosen = jax.random.randint(key_top, (), 0, USERS)
    return jnp.where(jnp.arange(USERS) == chosen, HEV, lengths).astype(jnp.int32)


def draw_candidates(key, part):
    key = jax.random.fold_in(key, 11)
    key_base, key_column, key_row = jax.random.split(key, 3)
    col_scale = jnp.exp(jax.random.uniform(key_column, (D,), minval=math.log(0.3), maxval=math.log(3.0)))
    row_scale = jnp.exp(jax.random.uniform(key_row, (USERS, NCR, 1), minval=math.log(0.5), maxval=math.log(2.0)))
    raw_values = jax.random.normal(key_base, (USERS, NCR, D))
    shaped = jnp.clip(raw_values * col_scale * row_scale, -24.0, 24.0)
    return shaped.astype(jnp.float32).astype(jnp.bfloat16)


def place_ends(values, stream_key, low, top_value):
    longest = values.shape.index(max(values.shape))
    spots = []
    for shift in (0, 1):
        where = [jax.random.randint(jax.random.fold_in(stream_key, axis), (), 0, length) for axis, length in enumerate(values.shape)]
        where[longest] = (where[longest] + shift) % values.shape[longest]
        spots.append(tuple(where))
    return values.at[spots[0]].set(low).at[spots[1]].set(top_value)


def shard_levels(own_key, shape, pieces, least, top_value):
    def one(axis_at, parts):
        draws = jax.random.uniform(jax.random.fold_in(jax.random.fold_in(own_key, 6), axis_at), (parts,), jnp.float32, least / len(pieces), top_value / len(pieces))
        return jnp.repeat(jnp.exp(draws), shape[axis_at] // parts).reshape((-1,) + (1,) * (len(shape) - axis_at - 1))

    gain = one(*pieces[0])
    for cut in pieces[1:]:
        gain = gain * one(*cut)
    return gain


def centred(rng, extent, width, reach, cuts=(), kind=jnp.bfloat16):
    values = width * jax.random.normal(rng, extent, jnp.float32)
    if cuts:
        values = values * shard_levels(rng, extent, cuts, -0.22, 0.18)
    return jnp.clip(values, -reach, reach).astype(kind)


def setup_inputs(seed: int = 0) -> dict:
    key_of = jax.random.split(jax.random.key(seed), 10)
    candidates = draw_candidates(jax.random.fold_in(key_of[9], 71), 0)
    live_counts = place_ends(jax.random.randint(key_of[1], (USERS,), 1, NCR + 1), jax.random.fold_in(key_of[1], 1), 1, NCR).astype(jnp.int32)
    request_user = draw_request_user(jax.random.fold_in(key_of[9], 71), 0)
    score_slot = draw_score_slot(jax.random.fold_in(key_of[9], 71), 0)
    history_cache = centred(key_of[4], (USERS, HEV, 2 * H * HD), 1.0, 6.0, ((0, 32), (2, 4)))
    history_length = draw_history_length(jax.random.fold_in(key_of[9], 71), 0)
    input_weight = centred(key_of[6], (D, 4 * H * HD), D ** -0.5, 0.1875, ((1, 4),))
    time_bias = centred(key_of[7], (H, NBKT), 1.0, 4.0, ((0, 4),), jnp.float32)
    output_weight = centred(key_of[8], (H * HD, D), (H * HD) ** -0.5, 0.1875, ((0, 4),))
    return dict(candidates=candidates, live_counts=live_counts, request_user=request_user, score_slot=score_slot, history_cache=history_cache, history_length=history_length, input_weight=input_weight, time_bias=time_bias, output_weight=output_weight)


EPSILON = 1e-05

def bucket_of(distance, bucket_total):
    bucket = jnp.zeros(distance.shape, jnp.int32)
    for exponent in range(bucket_total - 1):
        bucket = bucket + (distance >= 2 ** exponent).astype(jnp.int32)
    return bucket

def rounded(values):
    return lax.optimization_barrier(values.astype(jnp.bfloat16)).astype(jnp.float32)

def reference(candidates, live_counts, request_user, score_slot, history_cache, history_length, input_weight, time_bias, output_weight):
    inv_scale = 1.0 / math.sqrt(HD)

    def score_request(request):
        user_id = request_user[request]
        hist_size = history_length[user_id]
        cand_rows = lax.dynamic_index_in_dim(candidates, request, 0, keepdims=False).astype(jnp.float32)
        row_mean = lax.optimization_barrier(jnp.mean(cand_rows, axis=-1, keepdims=True))
        row_var = lax.optimization_barrier(jnp.mean(jnp.square(cand_rows - row_mean), axis=-1, keepdims=True))
        normed = ((cand_rows - row_mean) * lax.rsqrt(row_var + EPSILON)).astype(jnp.bfloat16)
        projected = jax.nn.silu(jnp.dot(normed, input_weight, preferred_element_type=jnp.float32))
        projected = rounded(projected).reshape(NCR, H, 4, HD)
        gate_part = projected[:, :, 0]
        values = projected[:, :, 1]
        queries = projected[:, :, 2]
        key_part = projected[:, :, 3]
        history_kv = lax.dynamic_index_in_dim(history_cache, user_id, 0, keepdims=False)
        history_kv = history_kv.astype(jnp.float32).reshape(HEV, H, 2, HD)
        positions = jnp.arange(HEV, dtype=jnp.int32)
        row_bias = time_bias[:, bucket_of(hist_size - positions, NBKT)]
        scores = jnp.einsum('chd,thd->hct', queries, history_kv[:, :, 0]) * inv_scale + row_bias[:, None, :]
        divisor = (hist_size + 1).astype(jnp.float32)
        is_live = (positions < hist_size)[None, None, :]
        weights = rounded(jnp.where(is_live, jax.nn.silu(scores) / divisor, 0.0))
        history = jnp.einsum('hct,thd->chd', weights, history_kv[:, :, 1])
        self_score = lax.optimization_barrier(jnp.sum(queries * key_part, axis=-1)) * inv_scale + time_bias[:, 0][None, :]
        self_weight = rounded(jax.nn.silu(self_score) / divisor)
        combined = history + self_weight[..., None] * values
        head_mean = lax.optimization_barrier(jnp.mean(combined, axis=-1, keepdims=True))
        head_var = lax.optimization_barrier(jnp.mean(jnp.square(combined - head_mean), axis=-1, keepdims=True))
        gated_rows = ((combined - head_mean) * lax.rsqrt(head_var + EPSILON) * gate_part).reshape(NCR, H * HD).astype(jnp.bfloat16)
        result = jnp.dot(gated_rows, output_weight, preferred_element_type=jnp.float32) + cand_rows
        alive_mask = jnp.arange(NCR, dtype=jnp.int32) < live_counts[request]
        return jnp.where(alive_mask[:, None], result, 0.0).astype(jnp.bfloat16)
    scored = lax.map(score_request, jnp.arange(USERS, dtype=jnp.int32))
    return jnp.zeros_like(scored).at[score_slot[request_user]].set(scored)
```

```python
import math

import jax
import jax.numpy as jnp
from jax import lax
from jax.experimental import pallas as pl
from jax.experimental.pallas import tpu as pltpu
from jax.sharding import PartitionSpec as P

HD = 128
EPSILON = 1e-05
VMEM = 48 * 1024 * 1024

PIECES = ((0, 128),)
BATCH = 4


def permute_out(index, parts, out_rows, pieces):
    users = parts[0].shape[0]
    width = parts[0].shape[2]

    def body(index_ref, *refs):
        ins, out, sem = refs[: len(parts)], refs[len(parts)], refs[len(parts) + 1]

        def copy(i, c):
            start, size = pieces[c]
            return pltpu.make_async_copy(
                ins[c].at[i], out.at[index_ref[i], pl.ds(start, size)], sem.at[c, i]
            )

        for c in range(len(parts)):
            for i in range(users):
                copy(i, c).start()
        for c in range(len(parts)):
            for i in range(users):
                copy(i, c).wait()

    return pl.pallas_call(
        body,
        out_shape=jax.ShapeDtypeStruct((users, out_rows, width), parts[0].dtype),
        in_specs=[pl.BlockSpec(memory_space=pltpu.SMEM)]
        + [pl.BlockSpec(memory_space=pl.ANY)] * len(parts),
        out_specs=pl.BlockSpec(memory_space=pl.ANY),
        scratch_shapes=[pltpu.SemaphoreType.DMA((len(parts), users))],
    )(index, *parts)


def permute_in(index, whole, piece):
    users, _, width = whole.shape
    start, size = piece

    def body(index_ref, src, out, sem):
        def copy(i):
            return pltpu.make_async_copy(
                src.at[index_ref[i], pl.ds(start, size)], out.at[i], sem.at[i]
            )

        for i in range(users):
            copy(i).start()
        for i in range(users):
            copy(i).wait()

    return pl.pallas_call(
        body,
        out_shape=jax.ShapeDtypeStruct((users, size, width), whole.dtype),
        in_specs=[pl.BlockSpec(memory_space=pltpu.SMEM), pl.BlockSpec(memory_space=pl.ANY)],
        out_specs=pl.BlockSpec(memory_space=pl.ANY),
        scratch_shapes=[pltpu.SemaphoreType.DMA((users,))],
    )(index, whole)


def attend(full, weight, history, order, rows_info, heads):
    mp, users, rows, part = full.shape
    events, kv_width = history.shape[1:]
    quarter = rows // mp
    total = BATCH * rows
    inv_scale = 1.0 / math.sqrt(HD)

    def body(order_ref, full_ref, weight_ref, info_ref, *refs):
        hist_refs, out_ref = refs[:BATCH], refs[BATCH]
        parts = [full_ref[k].reshape(total, part).astype(jnp.float32) for k in range(mp)]
        width = mp * part
        mean = sum(jnp.sum(p, axis=-1, keepdims=True) for p in parts) * (1.0 / width)
        parts = [p - mean for p in parts]
        var = sum(jnp.sum(p * p, axis=-1, keepdims=True) for p in parts) * (1.0 / width)
        factor = lax.rsqrt(var + EPSILON)
        normed = jnp.concatenate([(p * factor).astype(jnp.bfloat16) for p in parts], axis=1)
        for h in range(heads):
            half = 0.5 * jnp.dot(
                normed,
                weight_ref[:, h * 4 * HD : (h + 1) * 4 * HD],
                preferred_element_type=jnp.float32,
            )
            projected = (half + half * jnp.tanh(half)).astype(jnp.bfloat16)
            for b in range(BATCH):
                mine = projected[b * rows : (b + 1) * rows]
                gate = mine[:, :HD].astype(jnp.float32)
                value = mine[:, HD : 2 * HD].astype(jnp.float32)
                query = mine[:, 2 * HD : 3 * HD]
                key = mine[:, 3 * HD :].astype(jnp.float32)
                cache_key = hist_refs[b][0, :, 2 * h * HD : (2 * h + 1) * HD]
                cache_value = hist_refs[b][0, :, (2 * h + 1) * HD : (2 * h + 2) * HD]
                score = lax.dot_general(
                    query, cache_key, (((1,), (1,)), ((), ())), preferred_element_type=jnp.float32
                )
                score = score * (0.5 * inv_scale) + info_ref[b, h : h + 1, :]
                weights = (score + score * jnp.tanh(score)) * info_ref[b, 2 * heads : 2 * heads + 1, :]
                summed = jnp.dot(
                    weights.astype(jnp.bfloat16), cache_value, preferred_element_type=jnp.float32
                )
                own = jnp.sum(query.astype(jnp.float32) * key, axis=-1, keepdims=True)
                own = own * (0.5 * inv_scale) + info_ref[b, heads + h : heads + h + 1, :HD]
                own = (own + own * jnp.tanh(own)) * info_ref[b, 2 * heads + 1 : 2 * heads + 2, :HD]
                own = own.astype(jnp.bfloat16).astype(jnp.float32)
                combined = summed + own * value
                head_mean = jnp.mean(combined, axis=-1, keepdims=True)
                centred = combined - head_mean
                head_var = jnp.mean(centred * centred, axis=-1, keepdims=True)
                gated = (centred * lax.rsqrt(head_var + EPSILON) * gate).astype(jnp.bfloat16)
                for q in range(mp):
                    out_ref[q, b, :, h * HD : (h + 1) * HD] = gated[q * quarter : (q + 1) * quarter]

    def hist_spec(b):
        return pl.BlockSpec((1, events, kv_width), lambda i, order: (order[i * BATCH + b], 0, 0))

    return pl.pallas_call(
        body,
        out_shape=jax.ShapeDtypeStruct((mp, users, quarter, heads * HD), jnp.bfloat16),
        grid_spec=pltpu.PrefetchScalarGridSpec(
            num_scalar_prefetch=1,
            grid=(users // BATCH,),
            in_specs=[
                pl.BlockSpec((mp, BATCH, rows, part), lambda i, order: (0, i, 0, 0)),
                pl.BlockSpec(weight.shape, lambda i, order: (0, 0)),
                pl.BlockSpec((BATCH,) + rows_info.shape[1:], lambda i, order: (i, 0, 0)),
            ]
            + [hist_spec(b) for b in range(BATCH)],
            out_specs=pl.BlockSpec(
                (mp, BATCH, quarter, heads * HD), lambda i, order: (0, i, 0, 0)
            ),
        ),
        compiler_params=pltpu.CompilerParams(vmem_limit_bytes=VMEM),
    )(order, full, weight, rows_info, *([history] * BATCH))


def project_out(gated, full, weight, scalars, start):
    mp, users, quarter, part = gated.shape
    out_part = weight.shape[2] // mp
    batch = 8

    def body(scalar_ref, gated_ref, full_ref, weight_ref, out_ref):
        first = pl.program_id(0) * batch
        acc = jnp.dot(
            gated_ref[0].reshape(batch * quarter, part),
            weight_ref[0],
            preferred_element_type=jnp.float32,
        )
        for k in range(1, mp):
            acc = acc + jnp.dot(
                gated_ref[k].reshape(batch * quarter, part),
                weight_ref[k],
                preferred_element_type=jnp.float32,
            )
        row = lax.broadcasted_iota(jnp.int32, (quarter, out_part), 0)
        row = row + (start + scalar_ref[0] * quarter)
        for b in range(batch):
            alive = row < scalar_ref[1 + first + b]
            for k in range(mp):
                mine = acc[b * quarter : (b + 1) * quarter, k * out_part : (k + 1) * out_part]
                mine = mine + full_ref[k, b].astype(jnp.float32)
                out_ref[b, k] = jnp.where(alive, mine, 0.0).astype(jnp.bfloat16)

    return pl.pallas_call(
        body,
        out_shape=jax.ShapeDtypeStruct((users, mp, quarter, out_part), jnp.bfloat16),
        grid_spec=pltpu.PrefetchScalarGridSpec(
            num_scalar_prefetch=1,
            grid=(users // batch,),
            in_specs=[
                pl.BlockSpec((mp, batch, quarter, part), lambda i, s: (0, i, 0, 0)),
                pl.BlockSpec((mp, batch, quarter, part), lambda i, s: (0, i, s[0], 0)),
                pl.BlockSpec(weight.shape, lambda i, s: (0, 0, 0)),
            ],
            out_specs=pl.BlockSpec((batch, mp, quarter, out_part), lambda i, s: (i, 0, 0, 0)),
        ),
        compiler_params=pltpu.CompilerParams(vmem_limit_bytes=VMEM),
    )(scalars, gated, full, weight)


def bucket_bias(distance, time_bias):
    bias = jnp.broadcast_to(time_bias[:, 0][:, None, None], time_bias.shape[:1] + distance.shape)
    for k in range(time_bias.shape[1] - 1):
        bias = jnp.where((distance >= 2**k)[None], time_bias[:, k + 1][:, None, None], bias)
    return bias


def per_device(
    candidates,
    live_counts,
    request_user,
    score_slot,
    history_cache,
    history_length,
    input_weight,
    time_bias,
    output_weight,
):
    dp_size = lax.axis_size("dp")
    dp_rank = lax.axis_index("dp")
    mp_rank = lax.axis_index("mp")
    users, slots, part = candidates.shape
    events = history_cache.shape[1]
    heads = time_bias.shape[0]
    ranks = jnp.arange(dp_size, dtype=jnp.int32)
    local = jnp.arange(users, dtype=jnp.int32)
    scorer = score_slot // users

    table = lax.all_gather(jnp.stack([request_user, live_counts]), "dp", axis=0, tiled=False)
    all_users = table[:, 0].reshape(-1)
    all_live = table[:, 1].reshape(-1)
    weight_out = lax.all_gather(output_weight, "mp", axis=0, tiled=False)

    target = jnp.take(scorer, request_user)
    send_first = jnp.sum(jnp.where(target[None, :] == ranks[:, None], local[None, :], 0), axis=1)
    scored_here = scorer.reshape(dp_size, users) == dp_rank
    ids = jnp.arange(dp_size * users, dtype=jnp.int32)
    mine = jnp.sum(jnp.where(scored_here, ids.reshape(dp_size, users), 0), axis=1)
    place = jnp.sum(
        jnp.where(scored_here, score_slot.reshape(dp_size, users), 0), axis=1
    ) - dp_rank * users
    send_second = (
        jnp.sum(jnp.where(all_users[None, :] == mine[:, None], ids[None, :], 0), axis=1) // users
    )
    own_scorer = lax.dynamic_slice_in_dim(scorer, dp_rank * users, users)
    order = jnp.sum(jnp.where(own_scorer[None, :] == ranks[:, None], local[None, :], 0), axis=1)
    owned = dp_rank * users + order
    live = jnp.sum(jnp.where(all_users[None, :] == owned[:, None], all_live[None, :], 0), axis=1)
    scalars = jnp.concatenate([mp_rank[None], live]).astype(jnp.int32)

    lengths = jnp.take(history_length, order)
    position = jnp.arange(events, dtype=jnp.int32)
    distance = lengths[:, None] - position[None, :]
    inverse = 1.0 / (lengths + 1).astype(jnp.float32)
    spread = jnp.broadcast_to(inverse[:, None], (users, events))
    bias = 0.5 * bucket_bias(distance, time_bias)
    own_bias = jnp.broadcast_to(0.5 * time_bias[:, 0][:, None, None], bias.shape)
    info = [bias[h] for h in range(heads)] + [own_bias[h] for h in range(heads)]
    info = info + [jnp.where(distance > 0, spread, 0.0), spread]
    info = info + [jnp.zeros_like(spread)] * (-len(info) % 8)
    rows_info = jnp.stack(info, axis=1)

    results = []
    for piece in PIECES:
        rows = permute_in(send_first, candidates, piece)
        rows = lax.all_to_all(rows, "dp", split_axis=0, concat_axis=0, tiled=True)
        rows = permute_in(send_second, rows, (0, piece[1]))
        rows = lax.all_to_all(rows, "dp", split_axis=0, concat_axis=0, tiled=True)
        full = lax.all_gather(rows, "mp", axis=0, tiled=False)
        gated = attend(full, input_weight, history_cache, order, rows_info, heads)
        gated = lax.all_to_all(gated, "mp", split_axis=0, concat_axis=0, tiled=True)
        done = project_out(gated, full, weight_out, scalars, piece[0])
        done = done.reshape((-1,) + done.shape[2:])
        done = lax.all_to_all(done, ("dp", "mp"), split_axis=0, concat_axis=0, tiled=True)
        results.append(done.reshape(users, piece[1], part))
    return permute_out(place, results, slots, PIECES)


def solution(mesh):
    in_specs = (
        P("dp", None, "mp"),
        P("dp"),
        P("dp"),
        P(),
        P("dp", None, "mp"),
        P("dp"),
        P(None, "mp"),
        P("mp", None),
        P("mp", None),
    )
    out_specs = P("dp", None, "mp")
    return jax.shard_map(
        per_device, mesh=mesh, in_specs=in_specs, out_specs=out_specs, check_vma=False
    )
```

```python
import math

import jax
import jax.numpy as jnp
from jax import lax
from jax.experimental import pallas as pl
from jax.experimental.pallas import tpu as pltpu
from jax.sharding import PartitionSpec as P

HD = 128
EPSILON = 1e-05
VMEM = 48 * 1024 * 1024

PIECES = ((0, 64), (64, 64))
BATCH = 8


def permute_out(index, parts, out_rows, pieces):
    users, _, width = parts[0].shape
    count = len(parts)

    def body(index_ref, *refs):
        ins, out = refs[:count], refs[count]
        buffers, sem_in, sem_out = refs[count + 1 : 2 * count + 1], refs[-2], refs[-1]

        def load(c, i):
            return pltpu.make_async_copy(ins[c].at[i], buffers[c].at[i], sem_in.at[c, i])

        def store(c, i):
            start, size = pieces[c]
            return pltpu.make_async_copy(
                buffers[c].at[i], out.at[index_ref[i], pl.ds(start, size)], sem_out.at[c, i]
            )

        every = [(c, i) for c in range(count) for i in range(users)]
        for c, i in every:
            load(c, i).start()
        for c, i in every:
            load(c, i).wait()
            store(c, i).start()
        for c, i in every:
            store(c, i).wait()

    return pl.pallas_call(
        body,
        out_shape=jax.ShapeDtypeStruct((users, out_rows, width), parts[0].dtype),
        in_specs=[pl.BlockSpec(memory_space=pltpu.SMEM)]
        + [pl.BlockSpec(memory_space=pl.ANY)] * count,
        out_specs=pl.BlockSpec(memory_space=pl.ANY),
        scratch_shapes=[pltpu.VMEM(p.shape, p.dtype) for p in parts]
        + [pltpu.SemaphoreType.DMA((count, users))] * 2,
        compiler_params=pltpu.CompilerParams(vmem_limit_bytes=VMEM),
    )(index, *parts)


def permute_in(index, whole, piece):
    users, _, width = whole.shape
    start, size = piece

    def body(index_ref, src, out, buffer, sem_in, sem_out):
        def load(i):
            return pltpu.make_async_copy(
                src.at[index_ref[i], pl.ds(start, size)], buffer.at[i], sem_in.at[i]
            )

        def store(i):
            return pltpu.make_async_copy(buffer.at[i], out.at[i], sem_out.at[i])

        for i in range(users):
            load(i).start()
        for i in range(users):
            load(i).wait()
            store(i).start()
        for i in range(users):
            store(i).wait()

    return pl.pallas_call(
        body,
        out_shape=jax.ShapeDtypeStruct((users, size, width), whole.dtype),
        in_specs=[pl.BlockSpec(memory_space=pltpu.SMEM), pl.BlockSpec(memory_space=pl.ANY)],
        out_specs=pl.BlockSpec(memory_space=pl.ANY),
        scratch_shapes=[pltpu.VMEM((users, size, width), whole.dtype)]
        + [pltpu.SemaphoreType.DMA((users,))] * 2,
        compiler_params=pltpu.CompilerParams(vmem_limit_bytes=VMEM),
    )(index, whole)


def attend(full, weight, history, order, rows_info, heads):
    mp, users, rows, part = full.shape
    events, kv_width = history.shape[1:]
    quarter = rows // mp
    total = BATCH * rows
    inv_scale = 1.0 / math.sqrt(HD)

    def body(order_ref, full_ref, weight_ref, info_ref, *refs):
        hist_refs, out_ref = refs[:BATCH], refs[BATCH]
        parts = [full_ref[k].reshape(total, part).astype(jnp.float32) for k in range(mp)]
        width = mp * part
        mean = sum(jnp.sum(p, axis=-1, keepdims=True) for p in parts) * (1.0 / width)
        parts = [p - mean for p in parts]
        var = sum(jnp.sum(p * p, axis=-1, keepdims=True) for p in parts) * (1.0 / width)
        factor = lax.rsqrt(var + EPSILON)
        normed = jnp.concatenate([(p * factor).astype(jnp.bfloat16) for p in parts], axis=1)
        for h in range(heads):
            half = 0.5 * jnp.dot(
                normed,
                weight_ref[:, h * 4 * HD : (h + 1) * 4 * HD],
                preferred_element_type=jnp.float32,
            )
            projected = (half + half * jnp.tanh(half)).astype(jnp.bfloat16)
            for b in range(BATCH):
                mine = projected[b * rows : (b + 1) * rows]
                gate = mine[:, :HD].astype(jnp.float32)
                value = mine[:, HD : 2 * HD].astype(jnp.float32)
                query = mine[:, 2 * HD : 3 * HD]
                key = mine[:, 3 * HD :].astype(jnp.float32)
                cache_key = hist_refs[b][0, :, 2 * h * HD : (2 * h + 1) * HD]
                cache_value = hist_refs[b][0, :, (2 * h + 1) * HD : (2 * h + 2) * HD]
                score = lax.dot_general(
                    query, cache_key, (((1,), (1,)), ((), ())), preferred_element_type=jnp.float32
                )
                score = score * (0.5 * inv_scale) + info_ref[b, h : h + 1, :]
                weights = (score + score * jnp.tanh(score)) * info_ref[b, 2 * heads : 2 * heads + 1, :]
                summed = jnp.dot(
                    weights.astype(jnp.bfloat16), cache_value, preferred_element_type=jnp.float32
                )
                own = jnp.sum(query.astype(jnp.float32) * key, axis=-1, keepdims=True)
                own = own * (0.5 * inv_scale) + info_ref[b, heads + h : heads + h + 1, :HD]
                own = (own + own * jnp.tanh(own)) * info_ref[b, 2 * heads + 1 : 2 * heads + 2, :HD]
                own = own.astype(jnp.bfloat16).astype(jnp.float32)
                combined = summed + own * value
                head_mean = jnp.mean(combined, axis=-1, keepdims=True)
                centred = combined - head_mean
                head_var = jnp.mean(centred * centred, axis=-1, keepdims=True)
                gated = (centred * lax.rsqrt(head_var + EPSILON) * gate).astype(jnp.bfloat16)
                for q in range(mp):
                    out_ref[q, b, :, h * HD : (h + 1) * HD] = gated[q * quarter : (q + 1) * quarter]

    def hist_spec(b):
        return pl.BlockSpec((1, events, kv_width), lambda i, order: (order[i * BATCH + b], 0, 0))

    return pl.pallas_call(
        body,
        out_shape=jax.ShapeDtypeStruct((mp, users, quarter, heads * HD), jnp.bfloat16),
        grid_spec=pltpu.PrefetchScalarGridSpec(
            num_scalar_prefetch=1,
            grid=(users // BATCH,),
            in_specs=[
                pl.BlockSpec((mp, BATCH, rows, part), lambda i, order: (0, i, 0, 0)),
                pl.BlockSpec(weight.shape, lambda i, order: (0, 0)),
                pl.BlockSpec((BATCH,) + rows_info.shape[1:], lambda i, order: (i, 0, 0)),
            ]
            + [hist_spec(b) for b in range(BATCH)],
            out_specs=pl.BlockSpec(
                (mp, BATCH, quarter, heads * HD), lambda i, order: (0, i, 0, 0)
            ),
        ),
        compiler_params=pltpu.CompilerParams(vmem_limit_bytes=VMEM),
    )(order, full, weight, rows_info, *([history] * BATCH))


def project_out(gated, full, weight, scalars, start):
    mp, users, quarter, part = gated.shape
    out_part = weight.shape[2] // mp
    batch = 8

    def body(scalar_ref, gated_ref, full_ref, weight_ref, out_ref):
        first = pl.program_id(0) * batch
        acc = jnp.dot(
            gated_ref[0].reshape(batch * quarter, part),
            weight_ref[0],
            preferred_element_type=jnp.float32,
        )
        for k in range(1, mp):
            acc = acc + jnp.dot(
                gated_ref[k].reshape(batch * quarter, part),
                weight_ref[k],
                preferred_element_type=jnp.float32,
            )
        row = lax.broadcasted_iota(jnp.int32, (quarter, out_part), 0)
        row = row + (start + scalar_ref[0] * quarter)
        for b in range(batch):
            alive = row < scalar_ref[1 + first + b]
            for k in range(mp):
                mine = acc[b * quarter : (b + 1) * quarter, k * out_part : (k + 1) * out_part]
                mine = mine + full_ref[k, b].astype(jnp.float32)
                out_ref[b, k] = jnp.where(alive, mine, 0.0).astype(jnp.bfloat16)

    return pl.pallas_call(
        body,
        out_shape=jax.ShapeDtypeStruct((users, mp, quarter, out_part), jnp.bfloat16),
        grid_spec=pltpu.PrefetchScalarGridSpec(
            num_scalar_prefetch=1,
            grid=(users // batch,),
            in_specs=[
                pl.BlockSpec((mp, batch, quarter, part), lambda i, s: (0, i, 0, 0)),
                pl.BlockSpec((mp, batch, quarter, part), lambda i, s: (0, i, s[0], 0)),
                pl.BlockSpec(weight.shape, lambda i, s: (0, 0, 0)),
            ],
            out_specs=pl.BlockSpec((batch, mp, quarter, out_part), lambda i, s: (i, 0, 0, 0)),
        ),
        compiler_params=pltpu.CompilerParams(vmem_limit_bytes=VMEM),
    )(scalars, gated, full, weight)


def bucket_bias(distance, time_bias):
    bias = jnp.broadcast_to(time_bias[:, 0][:, None, None], time_bias.shape[:1] + distance.shape)
    for k in range(time_bias.shape[1] - 1):
        bias = jnp.where((distance >= 2**k)[None], time_bias[:, k + 1][:, None, None], bias)
    return bias


def per_device(
    candidates,
    live_counts,
    request_user,
    score_slot,
    history_cache,
    history_length,
    input_weight,
    time_bias,
    output_weight,
):
    dp_size = lax.axis_size("dp")
    dp_rank = lax.axis_index("dp")
    mp_rank = lax.axis_index("mp")
    users, slots, part = candidates.shape
    events = history_cache.shape[1]
    heads = time_bias.shape[0]
    ranks = jnp.arange(dp_size, dtype=jnp.int32)
    local = jnp.arange(users, dtype=jnp.int32)
    scorer = score_slot // users

    own_table = jnp.stack([request_user, live_counts])
    table = lax.all_to_all(
        jnp.broadcast_to(own_table[None], (dp_size,) + own_table.shape),
        "dp",
        split_axis=0,
        concat_axis=0,
        tiled=True,
    )
    all_users = table[:, 0].reshape(-1)
    all_live = table[:, 1].reshape(-1)
    weight_out = lax.all_gather(output_weight, "mp", axis=0, tiled=False)

    target = jnp.take(scorer, request_user)
    send_first = jnp.sum(jnp.where(target[None, :] == ranks[:, None], local[None, :], 0), axis=1)
    scored_here = scorer.reshape(dp_size, users) == dp_rank
    ids = jnp.arange(dp_size * users, dtype=jnp.int32)
    mine = jnp.sum(jnp.where(scored_here, ids.reshape(dp_size, users), 0), axis=1)
    place = jnp.sum(
        jnp.where(scored_here, score_slot.reshape(dp_size, users), 0), axis=1
    ) - dp_rank * users
    send_second = (
        jnp.sum(jnp.where(all_users[None, :] == mine[:, None], ids[None, :], 0), axis=1) // users
    )
    own_scorer = lax.dynamic_slice_in_dim(scorer, dp_rank * users, users)
    order = jnp.sum(jnp.where(own_scorer[None, :] == ranks[:, None], local[None, :], 0), axis=1)
    owned = dp_rank * users + order
    live = jnp.sum(jnp.where(all_users[None, :] == owned[:, None], all_live[None, :], 0), axis=1)
    scalars = jnp.concatenate([mp_rank[None], live]).astype(jnp.int32)

    lengths = jnp.take(history_length, order)
    position = jnp.arange(events, dtype=jnp.int32)
    distance = lengths[:, None] - position[None, :]
    inverse = 1.0 / (lengths + 1).astype(jnp.float32)
    spread = jnp.broadcast_to(inverse[:, None], (users, events))
    bias = 0.5 * bucket_bias(distance, time_bias)
    own_bias = jnp.broadcast_to(0.5 * time_bias[:, 0][:, None, None], bias.shape)
    info = [bias[h] for h in range(heads)] + [own_bias[h] for h in range(heads)]
    info = info + [jnp.where(distance > 0, spread, 0.0), spread]
    info = info + [jnp.zeros_like(spread)] * (-len(info) % 8)
    rows_info = jnp.stack(info, axis=1)

    arrived = []
    before = None
    for piece in PIECES:
        rows = permute_in(send_first, candidates, piece)
        if before is not None:
            rows, before = lax.optimization_barrier((rows, before))
        rows = lax.all_to_all(rows, "dp", split_axis=0, concat_axis=0, tiled=True)
        rows = permute_in(send_second, rows, (0, piece[1]))
        before = lax.all_to_all(rows, "dp", split_axis=0, concat_axis=0, tiled=True)
        arrived.append(before)

    results = []
    for piece, rows in zip(PIECES, arrived):
        rows, weight_out = lax.optimization_barrier((rows, weight_out))
        full = lax.all_gather(rows, "mp", axis=0, tiled=False)
        gated = attend(full, input_weight, history_cache, order, rows_info, heads)
        gated = lax.all_to_all(gated, "mp", split_axis=0, concat_axis=0, tiled=True)
        done = project_out(gated, full, weight_out, scalars, piece[0])
        done = done.reshape((-1,) + done.shape[2:])
        done = lax.all_to_all(done, ("dp", "mp"), split_axis=0, concat_axis=0, tiled=True)
        results.append(done.reshape(users, piece[1], part))
    return permute_out(place, results, slots, PIECES)


def solution(mesh):
    in_specs = (
        P("dp", None, "mp"),
        P("dp"),
        P("dp"),
        P(),
        P("dp", None, "mp"),
        P("dp"),
        P(None, "mp"),
        P("mp", None),
        P("mp", None),
    )
    out_specs = P("dp", None, "mp")
    return jax.shard_map(
        per_device, mesh=mesh, in_specs=in_specs, out_specs=out_specs, check_vma=False
    )
```

```python
import math

import jax
import jax.numpy as jnp
from jax import lax
from jax.experimental import pallas as pl
from jax.experimental.pallas import tpu as pltpu
from jax.sharding import PartitionSpec as P

HD = 128
EPSILON = 1e-05
VMEM = 48 * 1024 * 1024

PIECES = ((0, 64), (64, 64))
BATCH = 8
SIZE = 1088
GROUP = 16


def permute_out(index, part, piece, out_rows, whole=None):
    users, _, width = part.shape
    start, size = piece

    def body(index_ref, src, *refs):
        out, sem = refs[-2:]

        def store(i):
            return pltpu.make_async_copy(
                src.at[i], out.at[index_ref[i], pl.ds(start, size)], sem.at[i]
            )

        for i in range(users):
            store(i).start()
        for i in range(users):
            store(i).wait()

    extra = () if whole is None else (whole,)
    return pl.pallas_call(
        body,
        out_shape=jax.ShapeDtypeStruct((users, out_rows, width), part.dtype),
        in_specs=[
            pl.BlockSpec(memory_space=pltpu.SMEM),
            pl.BlockSpec(memory_space=pltpu.VMEM),
        ]
        + [pl.BlockSpec(memory_space=pl.ANY)] * len(extra),
        out_specs=pl.BlockSpec(memory_space=pl.ANY),
        scratch_shapes=[pltpu.SemaphoreType.DMA((users,))],
        input_output_aliases={2: 0} if extra else {},
        compiler_params=pltpu.CompilerParams(vmem_limit_bytes=VMEM),
    )(index, part, *extra)


def permute_in(index, whole, piece, tags=()):
    users, _, width = whole.shape
    start, size = piece
    rows = size + GROUP if tags else size

    def body(index_ref, *refs):
        src, out = refs[-2:]
        upper = lax.broadcasted_iota(jnp.int32, (GROUP, width), 0) < GROUP // 2
        for i in range(users):
            at = index_ref[i]
            out[i, :size, :] = src[at, start : start + size, :]
            if tags:
                tag = jnp.where(upper, refs[0][at], refs[1][at])
                out[i, size:, :] = tag.astype(jnp.float32).astype(whole.dtype)

    return pl.pallas_call(
        body,
        out_shape=jax.ShapeDtypeStruct((users, rows, width), whole.dtype),
        in_specs=[pl.BlockSpec(memory_space=pltpu.SMEM)] * (1 + len(tags))
        + [pl.BlockSpec(memory_space=pltpu.VMEM)],
        out_specs=pl.BlockSpec(memory_space=pltpu.VMEM),
        compiler_params=pltpu.CompilerParams(vmem_limit_bytes=VMEM),
    )(index, *tags, whole)


def attend_batch(projected, caches, infos, h, heads):
    inv_scale = 1.0 / math.sqrt(HD)
    batch = len(projected)
    rows = projected[0].shape[0]
    scores = [
        lax.dot_general(
            p[:, 2 * HD : 3 * HD],
            cache[0],
            (((1,), (1,)), ((), ())),
            preferred_element_type=jnp.float32,
        )
        for p, cache in zip(projected, caches)
    ]
    scores = [s * (0.5 * inv_scale) + info[h : h + 1, :] for s, info in zip(scores, infos)]
    weights = [
        ((s + s * jnp.tanh(s)) * info[2 * heads : 2 * heads + 1, :]).astype(jnp.bfloat16)
        for s, info in zip(scores, infos)
    ]
    summed = [
        jnp.dot(w, cache[1], preferred_element_type=jnp.float32)
        for w, cache in zip(weights, caches)
    ]
    whole = jnp.concatenate(projected, axis=0)
    gate, value, query, key = [
        whole[:, k * HD : (k + 1) * HD].astype(jnp.float32) for k in range(4)
    ]
    inverse = jnp.concatenate(
        [
            jnp.broadcast_to(info[2 * heads + 1 : 2 * heads + 2, :HD], (rows, HD))
            for info in infos
        ],
        axis=0,
    )
    own = jnp.sum(query * key, axis=-1, keepdims=True)
    own = own * (0.5 * inv_scale) + infos[0][heads + h : heads + h + 1, :HD]
    own = (own + own * jnp.tanh(own)) * inverse
    own = own.astype(jnp.bfloat16).astype(jnp.float32)
    combined = jnp.concatenate(summed, axis=0) + own * value
    head_mean = jnp.mean(combined, axis=-1, keepdims=True)
    centred = combined - head_mean
    head_var = jnp.mean(centred * centred, axis=-1, keepdims=True)
    return (centred * lax.rsqrt(head_var + EPSILON) * gate).astype(jnp.bfloat16)


def spread_quarters(whole_ref, out_refs, rows, rank):
    mp = len(out_refs)
    quarter = rows // mp
    for k in range(mp):
        at = ((rank + k) % mp) * quarter
        for b in range(BATCH):
            out_refs[k][b] = whole_ref[pl.ds(pl.multiple_of(b * rows + at, GROUP), quarter), :]


def normalise(parts):
    parts = [p.astype(jnp.float32) for p in parts]
    width = len(parts) * parts[0].shape[1]
    mean = sum(jnp.sum(p, axis=-1, keepdims=True) for p in parts) * (1.0 / width)
    parts = [p - mean for p in parts]
    var = sum(jnp.sum(p * p, axis=-1, keepdims=True) for p in parts) * (1.0 / width)
    factor = lax.rsqrt(var + EPSILON)
    return jnp.concatenate([(p * factor).astype(jnp.bfloat16) for p in parts], axis=1)


def silu_dot(normed, weight):
    half = 0.5 * jnp.dot(normed, weight, preferred_element_type=jnp.float32)
    return (half + half * jnp.tanh(half)).astype(jnp.bfloat16)


def head_cache(hist_ref, h):
    return (
        hist_ref[0, :, 2 * h * HD : (2 * h + 1) * HD],
        hist_ref[0, :, (2 * h + 1) * HD : (2 * h + 2) * HD],
    )


def attend(full, weight, history, order, rank, rows_info, heads):
    mp, users, rows, part = full.shape
    events, kv_width = history.shape[1:]
    quarter = rows // mp
    total = BATCH * rows

    def body(order_ref, rank_ref, full_ref, weight_ref, info_ref, *refs):
        hist_refs, out_refs, store = refs[:BATCH], refs[BATCH : BATCH + mp], refs[-1]
        normed = normalise([full_ref[k].reshape(total, part) for k in range(mp)])
        infos = [info_ref.at[b] for b in range(BATCH)]
        for h in range(heads):
            projected = silu_dot(normed, weight_ref[:, h * 4 * HD : (h + 1) * 4 * HD])
            store[:, h * HD : (h + 1) * HD] = attend_batch(
                [projected[b * rows : (b + 1) * rows] for b in range(BATCH)],
                [head_cache(hist_refs[b], h) for b in range(BATCH)],
                infos,
                h,
                heads,
            )
        spread_quarters(store, out_refs, rows, rank_ref[0])

    def hist_spec(b):
        return pl.BlockSpec((1, events, kv_width), lambda i, order, _: (order[i * BATCH + b], 0, 0))

    width = heads * HD
    return pl.pallas_call(
        body,
        out_shape=[jax.ShapeDtypeStruct((users, quarter, width), jnp.bfloat16)] * mp,
        grid_spec=pltpu.PrefetchScalarGridSpec(
            num_scalar_prefetch=2,
            grid=(users // BATCH,),
            in_specs=[
                pl.BlockSpec((mp, BATCH, rows, part), lambda i, *_: (0, i, 0, 0)),
                pl.BlockSpec(weight.shape, lambda i, *_: (0, 0)),
                pl.BlockSpec((BATCH,) + rows_info.shape[1:], lambda i, *_: (i, 0, 0)),
            ]
            + [hist_spec(b) for b in range(BATCH)],
            out_specs=[pl.BlockSpec((BATCH, quarter, width), lambda i, *_: (i, 0, 0))] * mp,
            scratch_shapes=[pltpu.VMEM((total, width), jnp.bfloat16)],
        ),
        compiler_params=pltpu.CompilerParams(vmem_limit_bytes=VMEM),
    )(order, rank, full, weight, rows_info, *([history] * BATCH))


def pack(slots, offsets, rows, size):
    users, count, width = rows.shape

    def body(slots_ref, offsets_ref, rows_ref, out, buffer, sem):
        for j in range(users):
            at = pl.multiple_of(offsets_ref[j], GROUP)
            buffer[pl.ds(at, count), :] = rows_ref[slots_ref[j]]
        copy = pltpu.make_async_copy(buffer.at[pl.ds(0, size)], out, sem)
        copy.start()
        copy.wait()

    return pl.pallas_call(
        body,
        out_shape=jax.ShapeDtypeStruct((size, width), rows.dtype),
        in_specs=[
            pl.BlockSpec(memory_space=pltpu.SMEM),
            pl.BlockSpec(memory_space=pltpu.SMEM),
            pl.BlockSpec(memory_space=pltpu.VMEM),
        ],
        out_specs=pl.BlockSpec(memory_space=pl.ANY),
        scratch_shapes=[
            pltpu.VMEM((size + count, width), rows.dtype),
            pltpu.SemaphoreType.DMA,
        ],
        compiler_params=pltpu.CompilerParams(vmem_limit_bytes=VMEM),
    )(slots, offsets, rows)


def attend_packed(
    full, weight, history, order, offsets, seats, last, rank, rows_info, rows, heads
):
    mp, size, part = full.shape
    users = order.shape[0]
    events, kv_width = history.shape[1:]
    quarter = rows // mp
    blocks = max(4, size // 256)
    block = size // blocks

    def body(
        order_ref, offsets_ref, seats_ref, last_ref, rank_ref, full_ref, weight_ref, info_ref, *refs
    ):
        hist_refs, out_refs = refs[:BATCH], refs[BATCH : BATCH + mp]
        store, merged = refs[-2:]
        step = pl.program_id(0)

        @pl.when(step < blocks)
        def _():
            normed = normalise([full_ref[k] for k in range(mp)])
            at = pl.multiple_of(step * block, GROUP)
            store[pl.ds(at, block), :] = silu_dot(normed, weight_ref[...])

        @pl.when((step >= blocks) & (step - blocks <= last_ref[0]))
        def _():
            seats = [(step - blocks) * BATCH + b for b in range(BATCH)]
            starts = [pl.multiple_of(offsets_ref[j], GROUP) for j in seats]
            infos = [info_ref.at[seats_ref[j]] for j in seats]
            for h in range(heads):
                merged[:, h * HD : (h + 1) * HD] = attend_batch(
                    [store[pl.ds(at, rows), h * 4 * HD : (h + 1) * 4 * HD] for at in starts],
                    [head_cache(hist_refs[b], h) for b in range(BATCH)],
                    infos,
                    h,
                    heads,
                )
            spread_quarters(merged, out_refs, rows, rank_ref[0])

    def batch_of(i):
        return jnp.maximum(i - blocks, 0)

    def hist_spec(b):
        return pl.BlockSpec(
            (1, events, kv_width),
            lambda i, order, offsets, seats, last, rank: (
                order[jnp.minimum(batch_of(i), last[0]) * BATCH + b],
                0,
                0,
            ),
        )

    width = heads * HD
    return pl.pallas_call(
        body,
        out_shape=[jax.ShapeDtypeStruct((users, quarter, width), jnp.bfloat16)] * mp,
        grid_spec=pltpu.PrefetchScalarGridSpec(
            num_scalar_prefetch=5,
            grid=(blocks + users // BATCH,),
            in_specs=[
                pl.BlockSpec(
                    (mp, block, part), lambda i, *_: (0, jnp.minimum(i, blocks - 1), 0)
                ),
                pl.BlockSpec(weight.shape, lambda i, *_: (0, 0)),
                pl.BlockSpec(rows_info.shape, lambda i, *_: (0, 0, 0)),
            ]
            + [hist_spec(b) for b in range(BATCH)],
            out_specs=[pl.BlockSpec((BATCH, quarter, width), lambda i, *_: (batch_of(i), 0, 0))]
            * mp,
            scratch_shapes=[
                pltpu.VMEM((size + rows, weight.shape[1]), jnp.bfloat16),
                pltpu.VMEM((BATCH * rows, width), jnp.bfloat16),
            ],
        ),
        compiler_params=pltpu.CompilerParams(vmem_limit_bytes=VMEM),
    )(order, offsets, seats, last, rank, full, weight, rows_info, *([history] * BATCH))


def rank_dot(gated, weights):
    terms = [
        jnp.dot(g, w, preferred_element_type=jnp.float32) for g, w in zip(gated, weights)
    ]
    return sum(terms[1:], terms[0])


def project_out(gated, full, weights, scalars, start):
    mp = len(gated)
    users, quarter, part = gated[0].shape
    out_part = weights[0].shape[1] // mp
    batch = 8

    def body(scalar_ref, full_ref, *refs):
        gated_refs, weight_refs, out_ref = refs[:mp], refs[mp : 2 * mp], refs[-1]
        first = pl.program_id(0) * batch
        acc = rank_dot(
            [g[...].reshape(batch * quarter, part) for g in gated_refs],
            [w[...] for w in weight_refs],
        )
        row = lax.broadcasted_iota(jnp.int32, (quarter, out_part), 0)
        row = row + (start + scalar_ref[0] * quarter)
        for b in range(batch):
            alive = row < scalar_ref[1 + first + b]
            for k in range(mp):
                mine = acc[b * quarter : (b + 1) * quarter, k * out_part : (k + 1) * out_part]
                mine = mine + full_ref[k, b].astype(jnp.float32)
                out_ref[b, k] = jnp.where(alive, mine, 0.0).astype(jnp.bfloat16)

    return pl.pallas_call(
        body,
        out_shape=jax.ShapeDtypeStruct((users, mp, quarter, out_part), jnp.bfloat16),
        grid_spec=pltpu.PrefetchScalarGridSpec(
            num_scalar_prefetch=1,
            grid=(users // batch,),
            in_specs=[pl.BlockSpec((mp, batch, quarter, part), lambda i, s: (0, i, s[0], 0))]
            + [pl.BlockSpec((batch, quarter, part), lambda i, s: (i, 0, 0)) for _ in gated]
            + [pl.BlockSpec(w.shape, lambda i, s: (0, 0)) for w in weights],
            out_specs=pl.BlockSpec((batch, mp, quarter, out_part), lambda i, s: (i, 0, 0, 0)),
        ),
        compiler_params=pltpu.CompilerParams(vmem_limit_bytes=VMEM),
    )(scalars, full, *gated, *weights)


def project_out_packed(gated, full, weights, scalars, slots, offsets, start):
    mp = len(gated)
    users, quarter, part = gated[0].shape
    size = full.shape[1]
    out_part = weights[0].shape[1] // mp

    def body(scalar_ref, slots_ref, offsets_ref, full_ref, *refs):
        gated_refs, weight_refs, out_ref = refs[:mp], refs[mp : 2 * mp], refs[-1]
        rank = scalar_ref[0]
        acc = rank_dot(
            [g[...].reshape(users * quarter, part) for g in gated_refs],
            [w[...] for w in weight_refs],
        )
        row = lax.broadcasted_iota(jnp.int32, (quarter, out_part), 0) + (start + rank * quarter)
        for j in range(users):
            at = jnp.minimum(offsets_ref[j] + rank * quarter, size - quarter)
            residual = full_ref[0, pl.ds(pl.multiple_of(at, GROUP), quarter), :]
            mine = acc[j * quarter : (j + 1) * quarter] + residual.astype(jnp.float32)
            alive = row < scalar_ref[1 + j]
            out_ref[slots_ref[j], 0] = jnp.where(alive, mine, 0.0).astype(jnp.bfloat16)

    return pl.pallas_call(
        body,
        out_shape=jax.ShapeDtypeStruct((users, mp, quarter, out_part), jnp.bfloat16),
        grid_spec=pltpu.PrefetchScalarGridSpec(
            num_scalar_prefetch=3,
            grid=(mp,),
            in_specs=[pl.BlockSpec((1, size, part), lambda i, *_: (i, 0, 0))]
            + [pl.BlockSpec((users, quarter, part), lambda i, *_: (0, 0, 0)) for _ in gated]
            + [pl.BlockSpec((part, out_part), lambda i, *_: (0, i)) for _ in weights],
            out_specs=pl.BlockSpec((users, 1, quarter, out_part), lambda i, *_: (0, i, 0, 0)),
        ),
        compiler_params=pltpu.CompilerParams(vmem_limit_bytes=VMEM),
    )(scalars, slots, offsets, full, *gated, *weights)


def bucket_bias(distance, time_bias):
    bias = jnp.broadcast_to(time_bias[:, 0][:, None, None], time_bias.shape[:1] + distance.shape)
    for k in range(time_bias.shape[1] - 1):
        bias = jnp.where((distance >= 2**k)[None], time_bias[:, k + 1][:, None, None], bias)
    return bias


def per_device(
    candidates,
    live_counts,
    request_user,
    score_slot,
    history_cache,
    history_length,
    input_weight,
    time_bias,
    output_weight,
):
    dp_size = lax.axis_size("dp")
    dp_rank = lax.axis_index("dp")
    mp_rank = lax.axis_index("mp")
    users, slots, part = candidates.shape
    events = history_cache.shape[1]
    heads = time_bias.shape[0]
    ranks = jnp.arange(dp_size, dtype=jnp.int32)
    local = jnp.arange(users, dtype=jnp.int32)
    scorer = score_slot // users

    target = jnp.take(scorer, request_user)
    send_first = jnp.sum(jnp.where(target[None, :] == ranks[:, None], local[None, :], 0), axis=1)
    def exchange(rows):
        return lax.all_to_all(rows, "dp", split_axis=0, concat_axis=0, tiled=True)

    mp_size = lax.axis_size("mp")

    def shifted(array, k):
        return lax.ppermute(array, "mp", [(i, (i + k) % mp_size) for i in range(mp_size)])

    first_rows, second_rows = PIECES[0][1], PIECES[1][1]
    weights_out = [output_weight] + [shifted(output_weight, k) for k in range(1, mp_size)]
    rows_0 = permute_in(send_first, candidates, PIECES[0], (request_user // users, live_counts))
    scored_0 = exchange(rows_0)
    owner_rank = scored_0[:, first_rows, 0].astype(jnp.int32)
    send_second = jnp.sum(
        jnp.where(owner_rank[None, :] == ranks[:, None], ranks[None, :], 0), axis=1
    )
    tagged_0 = exchange(permute_in(send_second, scored_0, (0, first_rows + GROUP)))
    owned_0 = tagged_0[:, :first_rows]
    live = tagged_0[:, first_rows + GROUP // 2, 0].astype(jnp.int32)

    scored_here = scorer.reshape(dp_size, users) == dp_rank
    place = jnp.sum(
        jnp.where(scored_here, score_slot.reshape(dp_size, users), 0), axis=1
    ) - dp_rank * users
    own_scorer = lax.dynamic_slice_in_dim(scorer, dp_rank * users, users)
    order = jnp.sum(jnp.where(own_scorer[None, :] == ranks[:, None], local[None, :], 0), axis=1)
    scalars = jnp.concatenate([mp_rank[None], live]).astype(jnp.int32)

    lengths = jnp.take(history_length, order)
    position = jnp.arange(events, dtype=jnp.int32)
    distance = lengths[:, None] - position[None, :]
    inverse = 1.0 / (lengths + 1).astype(jnp.float32)
    spread = jnp.broadcast_to(inverse[:, None], (users, events))
    bias = 0.5 * bucket_bias(distance, time_bias)
    own_bias = jnp.broadcast_to(0.5 * time_bias[:, 0][:, None, None], bias.shape)
    info = [bias[h] for h in range(heads)] + [own_bias[h] for h in range(heads)]
    info = info + [jnp.where(distance > 0, spread, 0.0), spread]
    info = info + [jnp.zeros_like(spread)] * (-len(info) % 8)
    rows_info = jnp.stack(info, axis=1)

    def padded(count):
        return (jnp.maximum(count - first_rows, 0) + (GROUP - 1)) // GROUP * GROUP

    groups = padded(live)
    has = groups > 0
    earlier = local[None, :] < local[:, None]
    count = jnp.sum(has.astype(jnp.int32))
    seat = jnp.where(
        has,
        jnp.sum((earlier & has[None, :]).astype(jnp.int32), axis=1),
        count + jnp.sum((earlier & ~has[None, :]).astype(jnp.int32), axis=1),
    )
    seated = seat[None, :] == local[:, None]

    def by_seat(values):
        return jnp.sum(jnp.where(seated, values[None, :], 0), axis=1).astype(jnp.int32)

    seat_slots = by_seat(local)
    seat_order = by_seat(order)
    seat_scalars = jnp.concatenate([mp_rank[None], by_seat(live)]).astype(jnp.int32)
    seat_offsets = jnp.sum(
        jnp.where(seat[None, :] < local[:, None], groups[None, :], 0), axis=1
    ).astype(jnp.int32)
    seat_offsets = jnp.minimum(seat_offsets, SIZE)
    rank = mp_rank[None].astype(jnp.int32)
    seat_last = (jnp.maximum(count - 1, 0) // BATCH)[None].astype(jnp.int32)

    def gather(rows):
        return lax.all_gather(rows, "mp", axis=0, tiled=False)

    def by_quarter(gated):
        return [gated[0]] + [shifted(gated[k], k) for k in range(1, mp_size)]

    def finish(done, size):
        done = done.reshape((-1,) + done.shape[2:])
        done = lax.all_to_all(done, ("dp", "mp"), split_axis=0, concat_axis=0, tiled=True)
        return done.reshape(users, size, part)

    def whole_piece(full, info, start):
        gated = attend(full, input_weight, history_cache, order, rank, info, heads)
        done = project_out(by_quarter(gated), full, weights_out, scalars, start)
        return finish(done, full.shape[2])

    rows_1 = permute_in(send_first, candidates, PIECES[1])
    rows_1, owned_0, rows_info, *weights_out = lax.optimization_barrier(
        (rows_1, owned_0, rows_info, *weights_out)
    )
    full_0 = gather(owned_0)
    owned_1 = exchange(permute_in(send_second, exchange(rows_1), (0, second_rows)))
    owned_1, full_0, groups = lax.optimization_barrier((owned_1, full_0, groups))
    packed = pack(seat_slots, seat_offsets, owned_1, SIZE)
    full_1 = gather(packed)
    own_most = jnp.broadcast_to(jnp.sum(groups).astype(jnp.int32)[None, None], (dp_size, 1))
    most = jnp.max(exchange(own_most))
    result_0 = whole_piece(full_0, rows_info, PIECES[0][0])
    gated_1 = attend_packed(
        full_1,
        input_weight,
        history_cache,
        seat_order,
        seat_offsets,
        seat_slots,
        seat_last,
        rank,
        rows_info,
        second_rows,
        heads,
    )
    done_1 = project_out_packed(
        by_quarter(gated_1),
        full_1,
        weights_out,
        seat_scalars,
        seat_slots,
        seat_offsets,
        PIECES[1][0],
    )
    result_1 = finish(done_1, second_rows)
    result_1 = lax.cond(
        most > SIZE,
        lambda ready, rows: whole_piece(gather(rows), rows_info, PIECES[1][0]),
        lambda ready, rows: ready,
        result_1,
        owned_1,
    )
    out = permute_out(place, result_0, PIECES[0], slots)
    return permute_out(place, result_1, PIECES[1], slots, out)


def solution(mesh):
    in_specs = (
        P("dp", None, "mp"),
        P("dp"),
        P("dp"),
        P(),
        P("dp", None, "mp"),
        P("dp"),
        P(None, "mp"),
        P("mp", None),
        P("mp", None),
    )
    out_specs = P("dp", None, "mp")
    return jax.shard_map(
        per_device, mesh=mesh, in_specs=in_specs, out_specs=out_specs, check_vma=False
    )
```

```python
import math

import jax
import jax.numpy as jnp
from jax import lax
from jax.experimental import pallas as pl
from jax.experimental.pallas import tpu as pltpu
from jax.sharding import PartitionSpec as P

HD = 128
EPSILON = 1e-05
VMEM = 48 * 1024 * 1024

PIECES = ((0, 64), (64, 64))
BATCH = 8
SIZE = 1088
GROUP = 16


def permute_out(index, results):
    users, mp, pieces, quarter, width = results.shape
    rows = pieces * mp * quarter

    def body(index_ref, src, out, buffer, sem):
        def store(i):
            return pltpu.make_async_copy(buffer.at[i], out.at[index_ref[i]], sem.at[i])

        for i in range(users):
            for n in range(pieces):
                for q in range(mp):
                    at = (n * mp + q) * quarter
                    buffer[i, at : at + quarter, :] = src[i, q, n]
            store(i).start()
        for i in range(users):
            store(i).wait()

    return pl.pallas_call(
        body,
        out_shape=jax.ShapeDtypeStruct((users, rows, width), results.dtype),
        in_specs=[
            pl.BlockSpec(memory_space=pltpu.SMEM),
            pl.BlockSpec(memory_space=pltpu.VMEM),
        ],
        out_specs=pl.BlockSpec(memory_space=pl.ANY),
        scratch_shapes=[
            pltpu.VMEM((users, rows, width), results.dtype),
            pltpu.SemaphoreType.DMA((users,)),
        ],
        compiler_params=pltpu.CompilerParams(vmem_limit_bytes=VMEM),
    )(index, results)


def permute_in(index, whole, piece, tags=()):
    users, _, width = whole.shape
    start, size = piece
    rows = size + GROUP if tags else size

    def body(index_ref, *refs):
        src, out = refs[-2:]
        upper = lax.broadcasted_iota(jnp.int32, (GROUP, width), 0) < GROUP // 2
        for i in range(users):
            at = index_ref[i]
            out[i, :size, :] = src[at, start : start + size, :]
            if tags:
                tag = jnp.where(upper, refs[0][at], refs[1][at])
                out[i, size:, :] = tag.astype(jnp.float32).astype(whole.dtype)

    return pl.pallas_call(
        body,
        out_shape=jax.ShapeDtypeStruct((users, rows, width), whole.dtype),
        in_specs=[pl.BlockSpec(memory_space=pltpu.SMEM)] * (1 + len(tags))
        + [pl.BlockSpec(memory_space=pltpu.VMEM)],
        out_specs=pl.BlockSpec(memory_space=pltpu.VMEM),
        compiler_params=pltpu.CompilerParams(vmem_limit_bytes=VMEM),
    )(index, *tags, whole)


def trim(rows, size):
    users, _, width = rows.shape

    def body(src, out):
        for i in range(users):
            out[i] = src[i, :size, :]

    return pl.pallas_call(
        body,
        out_shape=jax.ShapeDtypeStruct((users, size, width), rows.dtype),
        in_specs=[pl.BlockSpec(memory_space=pltpu.VMEM)],
        out_specs=pl.BlockSpec(memory_space=pltpu.VMEM),
        compiler_params=pltpu.CompilerParams(vmem_limit_bytes=VMEM),
    )(rows)


def attend_batch(projected, caches, infos, h, heads):
    inv_scale = 1.0 / math.sqrt(HD)
    batch = len(projected)
    rows = projected[0].shape[0]
    scores = [
        lax.dot_general(
            p[:, 2 * HD : 3 * HD],
            cache[0],
            (((1,), (1,)), ((), ())),
            preferred_element_type=jnp.float32,
        )
        for p, cache in zip(projected, caches)
    ]
    scores = [s * (0.5 * inv_scale) + info[h : h + 1, :] for s, info in zip(scores, infos)]
    weights = [
        ((s + s * jnp.tanh(s)) * info[2 * heads : 2 * heads + 1, :]).astype(jnp.bfloat16)
        for s, info in zip(scores, infos)
    ]
    summed = [
        jnp.dot(w, cache[1], preferred_element_type=jnp.float32)
        for w, cache in zip(weights, caches)
    ]
    whole = jnp.concatenate(projected, axis=0)
    gate, value, query, key = [
        whole[:, k * HD : (k + 1) * HD].astype(jnp.float32) for k in range(4)
    ]
    inverse = jnp.concatenate(
        [
            jnp.broadcast_to(info[2 * heads + 1 : 2 * heads + 2, :HD], (rows, HD))
            for info in infos
        ],
        axis=0,
    )
    own = jnp.sum(query * key, axis=-1, keepdims=True)
    own = own * (0.5 * inv_scale) + infos[0][heads + h : heads + h + 1, :HD]
    own = (own + own * jnp.tanh(own)) * inverse
    own = own.astype(jnp.bfloat16).astype(jnp.float32)
    combined = jnp.concatenate(summed, axis=0) + own * value
    head_mean = jnp.mean(combined, axis=-1, keepdims=True)
    centred = combined - head_mean
    head_var = jnp.mean(centred * centred, axis=-1, keepdims=True)
    return (centred * lax.rsqrt(head_var + EPSILON) * gate).astype(jnp.bfloat16)


def spread_quarters(whole_ref, out_refs, rows, rank):
    mp = len(out_refs)
    quarter = rows // mp
    for k in range(mp):
        at = ((rank + k) % mp) * quarter
        for b in range(BATCH):
            out_refs[k][b] = whole_ref[pl.ds(pl.multiple_of(b * rows + at, GROUP), quarter), :]


def normalise(parts):
    parts = [p.astype(jnp.float32) for p in parts]
    width = len(parts) * parts[0].shape[1]
    mean = sum(jnp.sum(p, axis=-1, keepdims=True) for p in parts) * (1.0 / width)
    parts = [p - mean for p in parts]
    var = sum(jnp.sum(p * p, axis=-1, keepdims=True) for p in parts) * (1.0 / width)
    factor = lax.rsqrt(var + EPSILON)
    return jnp.concatenate([(p * factor).astype(jnp.bfloat16) for p in parts], axis=1)


def silu_dot(normed, weight):
    half = 0.5 * jnp.dot(normed, weight, preferred_element_type=jnp.float32)
    return (half + half * jnp.tanh(half)).astype(jnp.bfloat16)


def head_cache(hist_ref, h):
    return (
        hist_ref[0, :, 2 * h * HD : (2 * h + 1) * HD],
        hist_ref[0, :, (2 * h + 1) * HD : (2 * h + 2) * HD],
    )


def attend(full, weight, history, order, rank, rows_info, heads, first, some, before=None):
    mp, users, rows, part = full.shape
    events, kv_width = history.shape[1:]
    quarter = rows // mp
    total = BATCH * rows
    width = heads * HD
    skip = first // BATCH

    def body(order_ref, rank_ref, full_ref, weight_ref, info_ref, *refs):
        hist_refs, out_refs, store = refs[:BATCH], refs[-1 - mp : -1], refs[-1]
        normed = normalise([full_ref[k].reshape(total, part) for k in range(mp)])
        infos = [info_ref.at[b] for b in range(BATCH)]
        for h in range(heads):
            projected = silu_dot(normed, weight_ref[:, h * 4 * HD : (h + 1) * 4 * HD])
            store[:, h * HD : (h + 1) * HD] = attend_batch(
                [projected[b * rows : (b + 1) * rows] for b in range(BATCH)],
                [head_cache(hist_refs[b], h) for b in range(BATCH)],
                infos,
                h,
                heads,
            )
        spread_quarters(store, out_refs, rows, rank_ref[0])

    def hist_spec(b):
        return pl.BlockSpec(
            (1, events, kv_width), lambda i, order, _: (order[(skip + i) * BATCH + b], 0, 0)
        )

    extra = () if before is None else tuple(before)
    inputs = (order, rank, full, weight, rows_info, *([history] * BATCH), *extra)
    at = len(inputs) - len(extra)
    return pl.pallas_call(
        body,
        out_shape=[jax.ShapeDtypeStruct((users, quarter, width), jnp.bfloat16)] * mp,
        grid_spec=pltpu.PrefetchScalarGridSpec(
            num_scalar_prefetch=2,
            grid=(some // BATCH,),
            in_specs=[
                pl.BlockSpec((mp, BATCH, rows, part), lambda i, *_: (0, skip + i, 0, 0)),
                pl.BlockSpec(weight.shape, lambda i, *_: (0, 0)),
                pl.BlockSpec((BATCH,) + rows_info.shape[1:], lambda i, *_: (skip + i, 0, 0)),
            ]
            + [hist_spec(b) for b in range(BATCH)]
            + [pl.BlockSpec(memory_space=pl.ANY) for _ in extra],
            out_specs=[pl.BlockSpec((BATCH, quarter, width), lambda i, *_: (skip + i, 0, 0))] * mp,
            scratch_shapes=[pltpu.VMEM((total, width), jnp.bfloat16)],
        ),
        input_output_aliases={at + k: k for k in range(len(extra))},
        compiler_params=pltpu.CompilerParams(vmem_limit_bytes=VMEM),
    )(*inputs)


def pack(slots, offsets, rows, size):
    users, count, width = rows.shape
    half = size // 2

    def body(slots_ref, offsets_ref, rows_ref, low, high, buffer):
        for j in range(users):
            at = pl.multiple_of(offsets_ref[j], GROUP)
            buffer[pl.ds(at, count), :] = rows_ref[slots_ref[j]]
        low[...] = buffer[:half, :]
        high[...] = buffer[half:size, :]

    return pl.pallas_call(
        body,
        out_shape=[jax.ShapeDtypeStruct((half, width), rows.dtype)] * 2,
        in_specs=[
            pl.BlockSpec(memory_space=pltpu.SMEM),
            pl.BlockSpec(memory_space=pltpu.SMEM),
            pl.BlockSpec(memory_space=pltpu.VMEM),
        ],
        out_specs=[pl.BlockSpec(memory_space=pltpu.VMEM)] * 2,
        scratch_shapes=[pltpu.VMEM((size + count, width), rows.dtype)],
        compiler_params=pltpu.CompilerParams(vmem_limit_bytes=VMEM),
    )(slots, offsets, rows)


def attend_packed(
    full, weight, history, order, offsets, seats, last, rank, rows_info, rows, heads
):
    mp = len(full)
    part = full[0][0].shape[1]
    size = sum(array.shape[0] for array in full[0])
    users = order.shape[0]
    events, kv_width = history.shape[1:]
    quarter = rows // mp
    blocks = 4
    block = size // blocks
    count = sum(len(arrays) for arrays in full)

    def body(
        order_ref, offsets_ref, seats_ref, last_ref, rank_ref, *refs
    ):
        weight_ref, info_ref = refs[count], refs[count + 1]
        hist_refs = refs[count + 2 : count + 2 + BATCH]
        out_refs = refs[count + 2 + BATCH : count + 2 + BATCH + mp]
        store, merged = refs[-2:]
        step = pl.program_id(0)

        @pl.when(step < blocks)
        def _():
            parts, at = [], 0
            for arrays in full:
                block_rows = refs[at][...]
                if len(arrays) > 1:
                    low = step < arrays[0].shape[0] // block
                    block_rows = jnp.where(low, block_rows, refs[at + 1][...])
                parts.append(block_rows)
                at = at + len(arrays)
            normed = normalise(parts)
            at = pl.multiple_of(step * block, GROUP)
            store[pl.ds(at, block), :] = silu_dot(normed, weight_ref[...])

        @pl.when((step >= blocks) & (step - blocks <= last_ref[0]))
        def _():
            seats = [(step - blocks) * BATCH + b for b in range(BATCH)]
            starts = [pl.multiple_of(offsets_ref[j], GROUP) for j in seats]
            infos = [info_ref.at[seats_ref[j]] for j in seats]
            for h in range(heads):
                merged[:, h * HD : (h + 1) * HD] = attend_batch(
                    [store[pl.ds(at, rows), h * 4 * HD : (h + 1) * 4 * HD] for at in starts],
                    [head_cache(hist_refs[b], h) for b in range(BATCH)],
                    infos,
                    h,
                    heads,
                )
            spread_quarters(merged, out_refs, rows, rank_ref[0])

    def full_spec(array, n):
        steps = array.shape[0] // block
        return pl.BlockSpec((block, part), lambda i, *_: (jnp.clip(i - n * steps, 0, steps - 1), 0))

    def batch_of(i):
        return jnp.maximum(i - blocks, 0)

    def hist_spec(b):
        return pl.BlockSpec(
            (1, events, kv_width),
            lambda i, order, offsets, seats, last, rank: (
                order[jnp.minimum(batch_of(i), last[0]) * BATCH + b],
                0,
                0,
            ),
        )

    width = heads * HD
    return pl.pallas_call(
        body,
        out_shape=[jax.ShapeDtypeStruct((users, quarter, width), jnp.bfloat16)] * mp,
        grid_spec=pltpu.PrefetchScalarGridSpec(
            num_scalar_prefetch=5,
            grid=(blocks + users // BATCH,),
            in_specs=[full_spec(array, n) for arrays in full for n, array in enumerate(arrays)]
            + [
                pl.BlockSpec(weight.shape, lambda i, *_: (0, 0)),
                pl.BlockSpec(rows_info.shape, lambda i, *_: (0, 0, 0)),
            ]
            + [hist_spec(b) for b in range(BATCH)],
            out_specs=[pl.BlockSpec((BATCH, quarter, width), lambda i, *_: (batch_of(i), 0, 0))]
            * mp,
            scratch_shapes=[
                pltpu.VMEM((size + rows, weight.shape[1]), jnp.bfloat16),
                pltpu.VMEM((BATCH * rows, width), jnp.bfloat16),
            ],
        ),
        compiler_params=pltpu.CompilerParams(vmem_limit_bytes=VMEM),
    )(order, offsets, seats, last, rank, *sum(full, []), weight, rows_info, *([history] * BATCH))


def rank_dot(gated, weights):
    terms = [
        jnp.dot(g, w, preferred_element_type=jnp.float32) for g, w in zip(gated, weights)
    ]
    return sum(terms[1:], terms[0])


def project_out(gated, full, weights, scalars, piece, before=None):
    mp = len(gated)
    users, quarter, part = gated[0].shape
    out_part = weights[0].shape[1] // mp
    batch = 8
    start = PIECES[piece][0]
    extra = () if before is None else (before,)

    def body(scalar_ref, full_ref, *refs):
        gated_refs, weight_refs, out_ref = refs[:mp], refs[mp : 2 * mp], refs[-1]
        first = pl.program_id(0) * batch
        acc = rank_dot(
            [g[...].reshape(batch * quarter, part) for g in gated_refs],
            [w[...] for w in weight_refs],
        )
        row = lax.broadcasted_iota(jnp.int32, (quarter, out_part), 0)
        row = row + (start + scalar_ref[0] * quarter)
        for b in range(batch):
            alive = row < scalar_ref[1 + first + b]
            for k in range(mp):
                mine = acc[b * quarter : (b + 1) * quarter, k * out_part : (k + 1) * out_part]
                mine = mine + full_ref[k, b].astype(jnp.float32)
                out_ref[b, k, 0] = jnp.where(alive, mine, 0.0).astype(jnp.bfloat16)

    return pl.pallas_call(
        body,
        out_shape=jax.ShapeDtypeStruct((users, mp, len(PIECES), quarter, out_part), jnp.bfloat16),
        grid_spec=pltpu.PrefetchScalarGridSpec(
            num_scalar_prefetch=1,
            grid=(users // batch,),
            in_specs=[pl.BlockSpec((mp, batch, quarter, part), lambda i, s: (0, i, s[0], 0))]
            + [pl.BlockSpec((batch, quarter, part), lambda i, s: (i, 0, 0)) for _ in gated]
            + [pl.BlockSpec(w.shape, lambda i, s: (0, 0)) for w in weights]
            + [pl.BlockSpec(memory_space=pl.ANY) for _ in extra],
            out_specs=pl.BlockSpec(
                (batch, mp, 1, quarter, out_part), lambda i, s: (i, 0, piece, 0, 0)
            ),
        ),
        input_output_aliases={2 + 2 * mp: 0} if extra else {},
        compiler_params=pltpu.CompilerParams(vmem_limit_bytes=VMEM),
    )(scalars, full, *gated, *weights, *extra)


def project_out_packed(gated, full, weights, scalars, slots, offsets, piece, before):
    mp = len(gated)
    users, quarter, part = gated[0].shape
    size = sum(array.shape[0] for array in full[0])
    out_part = weights[0].shape[1] // mp
    start = PIECES[piece][0]
    count = sum(len(arrays) for arrays in full)

    def column_of(k, rank):
        return (rank + (mp - k)) % mp

    def body(scalar_ref, slots_ref, offsets_ref, *refs):
        gated_refs, weight_refs = refs[count : count + mp], refs[count + mp : count + 2 * mp]
        out_ref, whole = refs[-2], refs[-1]
        rank = scalar_ref[0]
        first = 0
        for k, arrays in enumerate(full):

            @pl.when(pl.program_id(0) == k)
            def _():
                at = 0
                for n, array in enumerate(arrays):
                    whole[at : at + array.shape[0], :] = refs[first + n][...]
                    at = at + array.shape[0]

            first = first + len(arrays)
        acc = rank_dot(
            [g[...].reshape(users * quarter, part) for g in gated_refs],
            [w[...] for w in weight_refs],
        )
        row = lax.broadcasted_iota(jnp.int32, (quarter, out_part), 0) + (start + rank * quarter)
        for j in range(users):
            at = jnp.minimum(offsets_ref[j] + rank * quarter, size - quarter)
            residual = whole[pl.ds(pl.multiple_of(at, GROUP), quarter), :]
            mine = acc[j * quarter : (j + 1) * quarter] + residual.astype(jnp.float32)
            alive = row < scalar_ref[1 + j]
            out_ref[slots_ref[j], 0, 0] = jnp.where(alive, mine, 0.0).astype(jnp.bfloat16)

    return pl.pallas_call(
        body,
        out_shape=jax.ShapeDtypeStruct((users, mp, len(PIECES), quarter, out_part), jnp.bfloat16),
        grid_spec=pltpu.PrefetchScalarGridSpec(
            num_scalar_prefetch=3,
            grid=(mp,),
            in_specs=[
                pl.BlockSpec(array.shape, lambda i, *_: (0, 0)) for arrays in full for array in arrays
            ]
            + [pl.BlockSpec((users, quarter, part), lambda i, *_: (0, 0, 0)) for _ in gated]
            + [
                pl.BlockSpec((part, out_part), lambda i, s, *_: (0, column_of(i, s[0])))
                for _ in weights
            ]
            + [pl.BlockSpec(memory_space=pl.ANY)],
            out_specs=pl.BlockSpec(
                (users, 1, 1, quarter, out_part),
                lambda i, s, *_: (0, column_of(i, s[0]), piece, 0, 0),
            ),
            scratch_shapes=[pltpu.VMEM((size, part), jnp.bfloat16)],
        ),
        input_output_aliases={3 + count + 2 * mp: 0},
        compiler_params=pltpu.CompilerParams(vmem_limit_bytes=VMEM),
    )(scalars, slots, offsets, *sum(full, []), *gated, *weights, before)


def bucket_bias(distance, time_bias):
    bias = jnp.broadcast_to(time_bias[:, 0][:, None, None], time_bias.shape[:1] + distance.shape)
    for k in range(time_bias.shape[1] - 1):
        bias = jnp.where((distance >= 2**k)[None], time_bias[:, k + 1][:, None, None], bias)
    return bias


def per_device(
    candidates,
    live_counts,
    request_user,
    score_slot,
    history_cache,
    history_length,
    input_weight,
    time_bias,
    output_weight,
):
    dp_size = lax.axis_size("dp")
    dp_rank = lax.axis_index("dp")
    mp_rank = lax.axis_index("mp")
    users, slots, part = candidates.shape
    events = history_cache.shape[1]
    heads = time_bias.shape[0]
    ranks = jnp.arange(dp_size, dtype=jnp.int32)
    local = jnp.arange(users, dtype=jnp.int32)
    scorer = score_slot // users

    target = jnp.take(scorer, request_user)
    send_first = jnp.sum(jnp.where(target[None, :] == ranks[:, None], local[None, :], 0), axis=1)
    def exchange(rows):
        return lax.all_to_all(rows, "dp", split_axis=0, concat_axis=0, tiled=True)

    mp_size = lax.axis_size("mp")

    def shifted(array, k):
        return lax.ppermute(array, "mp", [(i, (i + k) % mp_size) for i in range(mp_size)])

    first_rows, second_rows = PIECES[0][1], PIECES[1][1]
    weights_out = [output_weight] + [shifted(output_weight, k) for k in range(1, mp_size)]
    rows_0 = permute_in(send_first, candidates, PIECES[0], (request_user // users, live_counts))
    scored_0 = exchange(rows_0)
    owner_rank = scored_0[:, first_rows, 0].astype(jnp.int32)
    send_second = jnp.sum(
        jnp.where(owner_rank[None, :] == ranks[:, None], ranks[None, :], 0), axis=1
    )
    tagged_0 = exchange(permute_in(send_second, scored_0, (0, first_rows + GROUP)))
    owned_0 = trim(tagged_0, first_rows)
    live = tagged_0[:, first_rows + GROUP // 2, 0].astype(jnp.int32)

    scored_here = scorer.reshape(dp_size, users) == dp_rank
    place = jnp.sum(
        jnp.where(scored_here, score_slot.reshape(dp_size, users), 0), axis=1
    ) - dp_rank * users
    own_scorer = lax.dynamic_slice_in_dim(scorer, dp_rank * users, users)
    order = jnp.sum(jnp.where(own_scorer[None, :] == ranks[:, None], local[None, :], 0), axis=1)
    scalars = jnp.concatenate([mp_rank[None], live]).astype(jnp.int32)

    lengths = jnp.take(history_length, order)
    position = jnp.arange(events, dtype=jnp.int32)
    distance = lengths[:, None] - position[None, :]
    inverse = 1.0 / (lengths + 1).astype(jnp.float32)
    spread = jnp.broadcast_to(inverse[:, None], (users, events))
    bias = 0.5 * bucket_bias(distance, time_bias)
    own_bias = jnp.broadcast_to(0.5 * time_bias[:, 0][:, None, None], bias.shape)
    info = [bias[h] for h in range(heads)] + [own_bias[h] for h in range(heads)]
    info = info + [jnp.where(distance > 0, spread, 0.0), spread]
    info = info + [jnp.zeros_like(spread)] * (-len(info) % 8)
    rows_info = jnp.stack(info, axis=1)

    def padded(count):
        return (jnp.maximum(count - first_rows, 0) + (GROUP - 1)) // GROUP * GROUP

    groups = padded(live)
    has = groups > 0
    earlier = local[None, :] < local[:, None]
    count = jnp.sum(has.astype(jnp.int32))
    seat = jnp.where(
        has,
        jnp.sum((earlier & has[None, :]).astype(jnp.int32), axis=1),
        count + jnp.sum((earlier & ~has[None, :]).astype(jnp.int32), axis=1),
    )
    seated = seat[None, :] == local[:, None]

    def by_seat(values):
        return jnp.sum(jnp.where(seated, values[None, :], 0), axis=1).astype(jnp.int32)

    seat_slots = by_seat(local)
    seat_order = by_seat(order)
    seat_scalars = jnp.concatenate([mp_rank[None], by_seat(live)]).astype(jnp.int32)
    seat_offsets = jnp.sum(
        jnp.where(seat[None, :] < local[:, None], groups[None, :], 0), axis=1
    ).astype(jnp.int32)
    seat_offsets = jnp.minimum(seat_offsets, SIZE)
    rank = mp_rank[None].astype(jnp.int32)
    seat_last = (jnp.maximum(count - 1, 0) // BATCH)[None].astype(jnp.int32)

    def gather(rows):
        return lax.all_gather(rows, "mp", axis=0, tiled=False)

    turned = (mp_rank + (mp_size - jnp.arange(mp_size, dtype=jnp.int32))) % mp_size
    weight_in = jnp.take(input_weight.reshape(mp_size, part, -1), turned, axis=0)
    weight_in = weight_in.reshape(input_weight.shape)

    def by_quarter(gated):
        return [gated[0]] + [shifted(gated[k], k) for k in range(1, mp_size)]

    rows_1 = permute_in(send_first, candidates, PIECES[1])
    rows_1, owned_0, rows_info, weight_in, *weights_out = lax.optimization_barrier(
        (rows_1, owned_0, rows_info, weight_in, *weights_out)
    )
    full_0 = gather(owned_0)
    owned_1 = exchange(permute_in(send_second, exchange(rows_1), (0, second_rows)))
    owned_1, groups = lax.optimization_barrier((owned_1, groups))
    packed = pack(seat_slots, seat_offsets, owned_1, SIZE)
    (low, high), full_0 = lax.optimization_barrier((packed, full_0))

    low_1, high_3 = shifted(low, 1), shifted(high, 3)
    high_1, low_3 = shifted(high, 1), shifted(low, 3)
    half = users // 2

    def attend_some(full, first, some, before=None):
        return attend(
            full, input_weight, history_cache, order, rank, rows_info, heads, first, some, before
        )

    gated_0 = attend_some(full_0, 0, half)
    low_1, high_3, gated_0 = lax.optimization_barrier((low_1, high_3, gated_0))
    low_2, high_2 = shifted(low_1, 1), shifted(high_3, 3)
    gated_0 = attend_some(full_0, half, users - half, gated_0)
    full_1 = [[low, high], [low_1, high_1], [low_2, high_2], [low_3, high_3]]
    gated_1 = attend_packed(
        full_1,
        weight_in,
        history_cache,
        seat_order,
        seat_offsets,
        seat_slots,
        seat_last,
        rank,
        rows_info,
        second_rows,
        heads,
    )
    done_0 = project_out(by_quarter(gated_0), full_0, weights_out, scalars, 0)
    done = project_out_packed(
        by_quarter(gated_1),
        full_1,
        weights_out,
        seat_scalars,
        seat_slots,
        seat_offsets,
        1,
        done_0,
    )

    def unpacked(done, rows):
        by_shift = jnp.stack([rows] + [shifted(rows, k) for k in range(1, mp_size)])
        full = jnp.take(by_shift, turned, axis=0)
        gated = by_quarter(attend_some(full, 0, users))
        return project_out(gated, full, weights_out, scalars, 1, done)

    done = lax.cond(
        jnp.sum(groups) > SIZE, unpacked, lambda done, rows: done, done, owned_1
    )
    results = lax.all_to_all(
        done.reshape((-1,) + done.shape[2:]), ("dp", "mp"), split_axis=0, concat_axis=0, tiled=True
    )
    return permute_out(place, results.reshape(done.shape))


def solution(mesh):
    in_specs = (
        P("dp", None, "mp"),
        P("dp"),
        P("dp"),
        P(),
        P("dp", None, "mp"),
        P("dp"),
        P(None, "mp"),
        P("mp", None),
        P("mp", None),
    )
    out_specs = P("dp", None, "mp")
    return jax.shard_map(
        per_device, mesh=mesh, in_specs=in_specs, out_specs=out_specs, check_vma=False
    )
```

```python
import math

import jax
import jax.numpy as jnp
from jax import lax
from jax.experimental import pallas as pl
from jax.experimental.pallas import tpu as pltpu
from jax.sharding import PartitionSpec as P

HD = 128
EPSILON = 1e-05
VMEM = 48 * 1024 * 1024

PIECES = ((0, 64), (64, 64))
BATCH = 8
SIZE = 1088
GROUP = 16


def permute_out(index, results):
    users, mp, pieces, quarter, width = results.shape
    rows = pieces * mp * quarter

    def body(index_ref, src, out, buffer, sem):
        def store(i):
            return pltpu.make_async_copy(buffer.at[i], out.at[index_ref[i]], sem.at[i])

        for i in range(users):
            for n in range(pieces):
                for q in range(mp):
                    at = (n * mp + q) * quarter
                    buffer[i, at : at + quarter, :] = src[i, q, n]
            store(i).start()
        for i in range(users):
            store(i).wait()

    return pl.pallas_call(
        body,
        out_shape=jax.ShapeDtypeStruct((users, rows, width), results.dtype),
        in_specs=[
            pl.BlockSpec(memory_space=pltpu.SMEM),
            pl.BlockSpec(memory_space=pltpu.VMEM),
        ],
        out_specs=pl.BlockSpec(memory_space=pl.ANY),
        scratch_shapes=[
            pltpu.VMEM((users, rows, width), results.dtype),
            pltpu.SemaphoreType.DMA((users,)),
        ],
        compiler_params=pltpu.CompilerParams(vmem_limit_bytes=VMEM),
    )(index, results)


def permute_in(index, whole, piece, tags=()):
    users, _, width = whole.shape
    start, size = piece
    rows = size + GROUP if tags else size

    def body(index_ref, *refs):
        src, out = refs[-2:]
        upper = lax.broadcasted_iota(jnp.int32, (GROUP, width), 0) < GROUP // 2
        for i in range(users):
            at = index_ref[i]
            out[i, :size, :] = src[at, start : start + size, :]
            if tags:
                tag = jnp.where(upper, refs[0][at], refs[1][at])
                out[i, size:, :] = tag.astype(jnp.float32).astype(whole.dtype)

    return pl.pallas_call(
        body,
        out_shape=jax.ShapeDtypeStruct((users, rows, width), whole.dtype),
        in_specs=[pl.BlockSpec(memory_space=pltpu.SMEM)] * (1 + len(tags))
        + [pl.BlockSpec(memory_space=pltpu.VMEM)],
        out_specs=pl.BlockSpec(memory_space=pltpu.VMEM),
        compiler_params=pltpu.CompilerParams(vmem_limit_bytes=VMEM),
    )(index, *tags, whole)


def halves(rows, size):
    users, _, width = rows.shape
    half = users // 2

    def body(src, *outs):
        for n in range(2):
            for i in range(half):
                outs[n][i] = src[n * half + i, :size, :]

    return pl.pallas_call(
        body,
        out_shape=[jax.ShapeDtypeStruct((half, size, width), rows.dtype)] * 2,
        in_specs=[pl.BlockSpec(memory_space=pltpu.VMEM)],
        out_specs=[pl.BlockSpec(memory_space=pltpu.VMEM)] * 2,
        compiler_params=pltpu.CompilerParams(vmem_limit_bytes=VMEM),
    )(rows)


def attend_batch(projected, caches, infos, h, heads):
    inv_scale = 1.0 / math.sqrt(HD)
    batch = len(projected)
    rows = projected[0].shape[0]
    scores = [
        lax.dot_general(
            p[:, 2 * HD : 3 * HD],
            cache[0],
            (((1,), (1,)), ((), ())),
            preferred_element_type=jnp.float32,
        )
        for p, cache in zip(projected, caches)
    ]
    scores = [s * (0.5 * inv_scale) + info[h : h + 1, :] for s, info in zip(scores, infos)]
    weights = [
        ((s + s * jnp.tanh(s)) * info[2 * heads : 2 * heads + 1, :]).astype(jnp.bfloat16)
        for s, info in zip(scores, infos)
    ]
    summed = [
        jnp.dot(w, cache[1], preferred_element_type=jnp.float32)
        for w, cache in zip(weights, caches)
    ]
    whole = jnp.concatenate(projected, axis=0)
    gate, value, query, key = [
        whole[:, k * HD : (k + 1) * HD].astype(jnp.float32) for k in range(4)
    ]
    inverse = jnp.concatenate(
        [
            jnp.broadcast_to(info[2 * heads + 1 : 2 * heads + 2, :HD], (rows, HD))
            for info in infos
        ],
        axis=0,
    )
    own = jnp.sum(query * key, axis=-1, keepdims=True)
    own = own * (0.5 * inv_scale) + infos[0][heads + h : heads + h + 1, :HD]
    own = (own + own * jnp.tanh(own)) * inverse
    own = own.astype(jnp.bfloat16).astype(jnp.float32)
    combined = jnp.concatenate(summed, axis=0) + own * value
    head_mean = jnp.mean(combined, axis=-1, keepdims=True)
    centred = combined - head_mean
    head_var = jnp.mean(centred * centred, axis=-1, keepdims=True)
    return (centred * lax.rsqrt(head_var + EPSILON) * gate).astype(jnp.bfloat16)


def spread_quarters(whole_ref, out_refs, rows, rank):
    mp = len(out_refs)
    quarter = rows // mp
    for k in range(mp):
        at = ((rank + k) % mp) * quarter
        for b in range(BATCH):
            out_refs[k][b] = whole_ref[pl.ds(pl.multiple_of(b * rows + at, GROUP), quarter), :]


def normalise(parts):
    parts = [p.astype(jnp.float32) for p in parts]
    width = len(parts) * parts[0].shape[1]
    mean = sum(jnp.sum(p, axis=-1, keepdims=True) for p in parts) * (1.0 / width)
    parts = [p - mean for p in parts]
    var = sum(jnp.sum(p * p, axis=-1, keepdims=True) for p in parts) * (1.0 / width)
    factor = lax.rsqrt(var + EPSILON)
    return jnp.concatenate([(p * factor).astype(jnp.bfloat16) for p in parts], axis=1)


def silu_dot(normed, weight):
    half = 0.5 * jnp.dot(normed, weight, preferred_element_type=jnp.float32)
    return (half + half * jnp.tanh(half)).astype(jnp.bfloat16)


def head_cache(hist_ref, h):
    return (
        hist_ref[0, :, 2 * h * HD : (2 * h + 1) * HD],
        hist_ref[0, :, (2 * h + 1) * HD : (2 * h + 2) * HD],
    )


def attend(full, weight, history, order, rank, rows_info, heads, first, before):
    mp = len(full)
    some, rows, part = full[0].shape
    users = order.shape[0]
    events, kv_width = history.shape[1:]
    quarter = rows // mp
    total = BATCH * rows
    skip = first // BATCH
    width = heads * HD

    def body(order_ref, rank_ref, *refs):
        full_refs, weight_ref, info_ref = refs[:mp], refs[mp], refs[mp + 1]
        hist_refs = refs[mp + 2 : mp + 2 + BATCH]
        out_refs, store = refs[-1 - mp : -1], refs[-1]
        normed = normalise([f[...].reshape(total, part) for f in full_refs])
        infos = [info_ref.at[b] for b in range(BATCH)]
        for h in range(heads):
            projected = silu_dot(normed, weight_ref[:, h * 4 * HD : (h + 1) * 4 * HD])
            store[:, h * HD : (h + 1) * HD] = attend_batch(
                [projected[b * rows : (b + 1) * rows] for b in range(BATCH)],
                [head_cache(hist_refs[b], h) for b in range(BATCH)],
                infos,
                h,
                heads,
            )
        spread_quarters(store, out_refs, rows, rank_ref[0])

    def hist_spec(b):
        return pl.BlockSpec(
            (1, events, kv_width), lambda i, order, _: (order[(skip + i) * BATCH + b], 0, 0)
        )

    extra = () if before is None else tuple(before)
    inputs = (order, rank, *full, weight, rows_info, *([history] * BATCH), *extra)
    at = len(inputs) - len(extra)
    return pl.pallas_call(
        body,
        out_shape=[jax.ShapeDtypeStruct((users, quarter, width), jnp.bfloat16)] * mp,
        grid_spec=pltpu.PrefetchScalarGridSpec(
            num_scalar_prefetch=2,
            grid=(some // BATCH,),
            in_specs=[pl.BlockSpec((BATCH, rows, part), lambda i, *_: (i, 0, 0)) for _ in full]
            + [
                pl.BlockSpec(weight.shape, lambda i, *_: (0, 0)),
                pl.BlockSpec((BATCH,) + rows_info.shape[1:], lambda i, *_: (skip + i, 0, 0)),
            ]
            + [hist_spec(b) for b in range(BATCH)]
            + [pl.BlockSpec(memory_space=pl.ANY) for _ in extra],
            out_specs=[pl.BlockSpec((BATCH, quarter, width), lambda i, *_: (skip + i, 0, 0))] * mp,
            scratch_shapes=[pltpu.VMEM((total, width), jnp.bfloat16)],
        ),
        input_output_aliases={at + k: k for k in range(len(extra))},
        compiler_params=pltpu.CompilerParams(vmem_limit_bytes=VMEM),
    )(*inputs)


def pack(slots, offsets, rows, size):
    users, count, width = rows.shape
    half = size // 2

    def body(slots_ref, offsets_ref, rows_ref, low, high, buffer):
        for j in range(users):
            at = pl.multiple_of(offsets_ref[j], GROUP)
            buffer[pl.ds(at, count), :] = rows_ref[slots_ref[j]]
        low[...] = buffer[:half, :]
        high[...] = buffer[half:size, :]

    return pl.pallas_call(
        body,
        out_shape=[jax.ShapeDtypeStruct((half, width), rows.dtype)] * 2,
        in_specs=[
            pl.BlockSpec(memory_space=pltpu.SMEM),
            pl.BlockSpec(memory_space=pltpu.SMEM),
            pl.BlockSpec(memory_space=pltpu.VMEM),
        ],
        out_specs=[pl.BlockSpec(memory_space=pltpu.VMEM)] * 2,
        scratch_shapes=[pltpu.VMEM((size + count, width), rows.dtype)],
        compiler_params=pltpu.CompilerParams(vmem_limit_bytes=VMEM),
    )(slots, offsets, rows)


def attend_packed(
    full, weight, history, order, offsets, seats, last, rank, rows_info, rows, heads
):
    mp = len(full)
    part = full[0][0].shape[1]
    size = sum(array.shape[0] for array in full[0])
    users = order.shape[0]
    events, kv_width = history.shape[1:]
    quarter = rows // mp
    blocks = 4
    block = size // blocks
    count = sum(len(arrays) for arrays in full)

    def body(
        order_ref, offsets_ref, seats_ref, last_ref, rank_ref, *refs
    ):
        weight_ref, info_ref = refs[count], refs[count + 1]
        hist_refs = refs[count + 2 : count + 2 + BATCH]
        out_refs = refs[count + 2 + BATCH : count + 2 + BATCH + mp]
        store, merged = refs[-2:]
        step = pl.program_id(0)

        @pl.when(step < blocks)
        def _():
            parts, at = [], 0
            for arrays in full:
                block_rows = refs[at][...]
                if len(arrays) > 1:
                    low = step < arrays[0].shape[0] // block
                    block_rows = jnp.where(low, block_rows, refs[at + 1][...])
                parts.append(block_rows)
                at = at + len(arrays)
            normed = normalise(parts)
            at = pl.multiple_of(step * block, GROUP)
            store[pl.ds(at, block), :] = silu_dot(normed, weight_ref[...])

        @pl.when((step >= blocks) & (step - blocks <= last_ref[0]))
        def _():
            seats = [(step - blocks) * BATCH + b for b in range(BATCH)]
            starts = [pl.multiple_of(offsets_ref[j], GROUP) for j in seats]
            infos = [info_ref.at[seats_ref[j]] for j in seats]
            for h in range(heads):
                merged[:, h * HD : (h + 1) * HD] = attend_batch(
                    [store[pl.ds(at, rows), h * 4 * HD : (h + 1) * 4 * HD] for at in starts],
                    [head_cache(hist_refs[b], h) for b in range(BATCH)],
                    infos,
                    h,
                    heads,
                )
            spread_quarters(merged, out_refs, rows, rank_ref[0])

    def full_spec(array, n):
        steps = array.shape[0] // block
        return pl.BlockSpec((block, part), lambda i, *_: (jnp.clip(i - n * steps, 0, steps - 1), 0))

    def batch_of(i):
        return jnp.maximum(i - blocks, 0)

    def hist_spec(b):
        return pl.BlockSpec(
            (1, events, kv_width),
            lambda i, order, offsets, seats, last, rank: (
                order[jnp.minimum(batch_of(i), last[0]) * BATCH + b],
                0,
                0,
            ),
        )

    width = heads * HD
    return pl.pallas_call(
        body,
        out_shape=[jax.ShapeDtypeStruct((users, quarter, width), jnp.bfloat16)] * mp,
        grid_spec=pltpu.PrefetchScalarGridSpec(
            num_scalar_prefetch=5,
            grid=(blocks + users // BATCH,),
            in_specs=[full_spec(array, n) for arrays in full for n, array in enumerate(arrays)]
            + [
                pl.BlockSpec(weight.shape, lambda i, *_: (0, 0)),
                pl.BlockSpec(rows_info.shape, lambda i, *_: (0, 0, 0)),
            ]
            + [hist_spec(b) for b in range(BATCH)],
            out_specs=[pl.BlockSpec((BATCH, quarter, width), lambda i, *_: (batch_of(i), 0, 0))]
            * mp,
            scratch_shapes=[
                pltpu.VMEM((size + rows, weight.shape[1]), jnp.bfloat16),
                pltpu.VMEM((BATCH * rows, width), jnp.bfloat16),
            ],
        ),
        compiler_params=pltpu.CompilerParams(vmem_limit_bytes=VMEM),
    )(order, offsets, seats, last, rank, *sum(full, []), weight, rows_info, *([history] * BATCH))


def rank_dot(gated, weights):
    terms = [
        jnp.dot(g, w, preferred_element_type=jnp.float32) for g, w in zip(gated, weights)
    ]
    return sum(terms[1:], terms[0])


def project_out(gated, full, weights, scalars, piece, before=None):
    mp = len(gated)
    users, quarter, part = gated[0].shape
    out_part = weights[0].shape[1] // mp
    batch = 8
    per_half = users // 2 // batch
    start = PIECES[piece][0]
    extra = () if before is None else (before,)

    def body(scalar_ref, *refs):
        full_refs, gated_refs = refs[: 2 * mp], refs[2 * mp : 3 * mp]
        weight_refs, out_ref = refs[3 * mp : 4 * mp], refs[-1]
        step = pl.program_id(0)
        rank = scalar_ref[0]
        rows = [g[...].reshape(batch * quarter, part) for g in gated_refs]
        row = lax.broadcasted_iota(jnp.int32, (quarter, out_part), 0) + (start + rank * quarter)
        for k in range(mp):
            column = (rank + (mp - k)) % mp
            at = pl.multiple_of(column * out_part, out_part)
            acc = rank_dot(rows, [w[:, pl.ds(at, out_part)] for w in weight_refs])
            for b in range(batch):
                alive = row < scalar_ref[1 + step * batch + b]
                residual = jnp.where(step < per_half, full_refs[k][b], full_refs[mp + k][b])
                mine = acc[b * quarter : (b + 1) * quarter] + residual.astype(jnp.float32)
                out_ref[b, column, 0] = jnp.where(alive, mine, 0.0).astype(jnp.bfloat16)

    def full_spec(n):
        return pl.BlockSpec(
            (batch, quarter, part),
            lambda i, s: (jnp.clip(i - n * per_half, 0, per_half - 1), s[0], 0),
        )

    return pl.pallas_call(
        body,
        out_shape=jax.ShapeDtypeStruct((users, mp, len(PIECES), quarter, out_part), jnp.bfloat16),
        grid_spec=pltpu.PrefetchScalarGridSpec(
            num_scalar_prefetch=1,
            grid=(users // batch,),
            in_specs=[full_spec(n) for n in range(2) for _ in range(mp)]
            + [pl.BlockSpec((batch, quarter, part), lambda i, s: (i, 0, 0)) for _ in gated]
            + [pl.BlockSpec(w.shape, lambda i, s: (0, 0)) for w in weights]
            + [pl.BlockSpec(memory_space=pl.ANY) for _ in extra],
            out_specs=pl.BlockSpec(
                (batch, mp, 1, quarter, out_part), lambda i, s: (i, 0, piece, 0, 0)
            ),
        ),
        input_output_aliases={1 + 4 * mp: 0} if extra else {},
        compiler_params=pltpu.CompilerParams(vmem_limit_bytes=VMEM),
    )(scalars, *full[0], *full[1], *gated, *weights, *extra)


def project_out_packed(gated, full, weights, scalars, slots, offsets, piece, before):
    mp = len(gated)
    users, quarter, part = gated[0].shape
    size = sum(array.shape[0] for array in full[0])
    out_part = weights[0].shape[1] // mp
    start = PIECES[piece][0]
    count = sum(len(arrays) for arrays in full)

    def column_of(k, rank):
        return (rank + (mp - k)) % mp

    def body(scalar_ref, slots_ref, offsets_ref, *refs):
        gated_refs, weight_refs = refs[count : count + mp], refs[count + mp : count + 2 * mp]
        out_ref, whole = refs[-2], refs[-1]
        rank = scalar_ref[0]
        first = 0
        for k, arrays in enumerate(full):

            @pl.when(pl.program_id(0) == k)
            def _():
                at = 0
                for n, array in enumerate(arrays):
                    whole[at : at + array.shape[0], :] = refs[first + n][...]
                    at = at + array.shape[0]

            first = first + len(arrays)
        acc = rank_dot(
            [g[...].reshape(users * quarter, part) for g in gated_refs],
            [w[...] for w in weight_refs],
        )
        row = lax.broadcasted_iota(jnp.int32, (quarter, out_part), 0) + (start + rank * quarter)
        for j in range(users):
            at = jnp.minimum(offsets_ref[j] + rank * quarter, size - quarter)
            residual = whole[pl.ds(pl.multiple_of(at, GROUP), quarter), :]
            mine = acc[j * quarter : (j + 1) * quarter] + residual.astype(jnp.float32)
            alive = row < scalar_ref[1 + j]
            out_ref[slots_ref[j], 0, 0] = jnp.where(alive, mine, 0.0).astype(jnp.bfloat16)

    return pl.pallas_call(
        body,
        out_shape=jax.ShapeDtypeStruct((users, mp, len(PIECES), quarter, out_part), jnp.bfloat16),
        grid_spec=pltpu.PrefetchScalarGridSpec(
            num_scalar_prefetch=3,
            grid=(mp,),
            in_specs=[
                pl.BlockSpec(array.shape, lambda i, *_: (0, 0)) for arrays in full for array in arrays
            ]
            + [pl.BlockSpec((users, quarter, part), lambda i, *_: (0, 0, 0)) for _ in gated]
            + [
                pl.BlockSpec((part, out_part), lambda i, s, *_: (0, column_of(i, s[0])))
                for _ in weights
            ]
            + [pl.BlockSpec(memory_space=pl.ANY)],
            out_specs=pl.BlockSpec(
                (users, 1, 1, quarter, out_part),
                lambda i, s, *_: (0, column_of(i, s[0]), piece, 0, 0),
            ),
            scratch_shapes=[pltpu.VMEM((size, part), jnp.bfloat16)],
        ),
        input_output_aliases={3 + count + 2 * mp: 0},
        compiler_params=pltpu.CompilerParams(vmem_limit_bytes=VMEM),
    )(scalars, slots, offsets, *sum(full, []), *gated, *weights, before)


def bucket_bias(distance, time_bias):
    bias = jnp.broadcast_to(time_bias[:, 0][:, None, None], time_bias.shape[:1] + distance.shape)
    for k in range(time_bias.shape[1] - 1):
        bias = jnp.where((distance >= 2**k)[None], time_bias[:, k + 1][:, None, None], bias)
    return bias


def per_device(
    candidates,
    live_counts,
    request_user,
    score_slot,
    history_cache,
    history_length,
    input_weight,
    time_bias,
    output_weight,
):
    dp_size = lax.axis_size("dp")
    dp_rank = lax.axis_index("dp")
    mp_rank = lax.axis_index("mp")
    users, slots, part = candidates.shape
    events = history_cache.shape[1]
    heads = time_bias.shape[0]
    ranks = jnp.arange(dp_size, dtype=jnp.int32)
    local = jnp.arange(users, dtype=jnp.int32)
    scorer = score_slot // users

    target = jnp.take(scorer, request_user)
    send_first = jnp.sum(jnp.where(target[None, :] == ranks[:, None], local[None, :], 0), axis=1)
    def exchange(rows):
        return lax.all_to_all(rows, "dp", split_axis=0, concat_axis=0, tiled=True)

    mp_size = lax.axis_size("mp")

    def shifted(array, k):
        return lax.ppermute(array, "mp", [(i, (i + k) % mp_size) for i in range(mp_size)])

    first_rows, second_rows = PIECES[0][1], PIECES[1][1]
    weights_out = [output_weight] + [shifted(output_weight, k) for k in range(1, mp_size)]
    rows_0 = permute_in(send_first, candidates, PIECES[0], (request_user // users, live_counts))
    scored_0 = exchange(rows_0)
    owner_rank = scored_0[:, first_rows, 0].astype(jnp.int32)
    send_second = jnp.sum(
        jnp.where(owner_rank[None, :] == ranks[:, None], ranks[None, :], 0), axis=1
    )
    tagged_0 = exchange(permute_in(send_second, scored_0, (0, first_rows + GROUP)))
    owned_0 = halves(tagged_0, first_rows)
    live = tagged_0[:, first_rows + GROUP // 2, 0].astype(jnp.int32)

    scored_here = scorer.reshape(dp_size, users) == dp_rank
    place = jnp.sum(
        jnp.where(scored_here, score_slot.reshape(dp_size, users), 0), axis=1
    ) - dp_rank * users
    own_scorer = lax.dynamic_slice_in_dim(scorer, dp_rank * users, users)
    order = jnp.sum(jnp.where(own_scorer[None, :] == ranks[:, None], local[None, :], 0), axis=1)
    scalars = jnp.concatenate([mp_rank[None], live]).astype(jnp.int32)

    lengths = jnp.take(history_length, order)
    position = jnp.arange(events, dtype=jnp.int32)
    distance = lengths[:, None] - position[None, :]
    inverse = 1.0 / (lengths + 1).astype(jnp.float32)
    spread = jnp.broadcast_to(inverse[:, None], (users, events))
    bias = 0.5 * bucket_bias(distance, time_bias)
    own_bias = jnp.broadcast_to(0.5 * time_bias[:, 0][:, None, None], bias.shape)
    info = [bias[h] for h in range(heads)] + [own_bias[h] for h in range(heads)]
    info = info + [jnp.where(distance > 0, spread, 0.0), spread]
    info = info + [jnp.zeros_like(spread)] * (-len(info) % 8)
    rows_info = jnp.stack(info, axis=1)

    def padded(count):
        return (jnp.maximum(count - first_rows, 0) + (GROUP - 1)) // GROUP * GROUP

    groups = padded(live)
    has = groups > 0
    earlier = local[None, :] < local[:, None]
    count = jnp.sum(has.astype(jnp.int32))
    seat = jnp.where(
        has,
        jnp.sum((earlier & has[None, :]).astype(jnp.int32), axis=1),
        count + jnp.sum((earlier & ~has[None, :]).astype(jnp.int32), axis=1),
    )
    seated = seat[None, :] == local[:, None]

    def by_seat(values):
        return jnp.sum(jnp.where(seated, values[None, :], 0), axis=1).astype(jnp.int32)

    seat_slots = by_seat(local)
    seat_order = by_seat(order)
    seat_scalars = jnp.concatenate([mp_rank[None], by_seat(live)]).astype(jnp.int32)
    seat_offsets = jnp.sum(
        jnp.where(seat[None, :] < local[:, None], groups[None, :], 0), axis=1
    ).astype(jnp.int32)
    seat_offsets = jnp.minimum(seat_offsets, SIZE)
    rank = mp_rank[None].astype(jnp.int32)
    seat_last = (jnp.maximum(count - 1, 0) // BATCH)[None].astype(jnp.int32)

    turned = (mp_rank + (mp_size - jnp.arange(mp_size, dtype=jnp.int32))) % mp_size
    weight_in = jnp.take(input_weight.reshape(mp_size, part, -1), turned, axis=0)
    weight_in = weight_in.reshape(input_weight.shape)

    def by_quarter(gated):
        return [gated[0]] + [shifted(gated[k], k) for k in range(1, mp_size)]

    rows_1 = permute_in(send_first, candidates, PIECES[1])
    rows_1, owned_0, rows_info, weight_in, *weights_out = lax.optimization_barrier(
        (rows_1, owned_0, rows_info, weight_in, *weights_out)
    )
    low_0, high_0 = owned_0
    full_low = [low_0, shifted(low_0, 1), None, shifted(low_0, 3)]
    full_low[2] = shifted(full_low[1], 1)
    full_high = [high_0, shifted(high_0, 1), None, shifted(high_0, 3)]
    full_high[2] = shifted(full_high[3], 3)
    owned_1 = exchange(permute_in(send_second, exchange(rows_1), (0, second_rows)))
    owned_1, groups = lax.optimization_barrier((owned_1, groups))
    packed = pack(seat_slots, seat_offsets, owned_1, SIZE)
    low, high = packed

    def attend_some(full, first, before=None):
        return attend(
            full, weight_in, history_cache, order, rank, rows_info, heads, first, before
        )

    gated_low = attend_some(full_low, 0)
    low_1, high_3 = shifted(low, 1), shifted(high, 3)
    high_1, low_3 = shifted(high, 1), shifted(low, 3)
    low_1, high_3, gated_low = lax.optimization_barrier((low_1, high_3, gated_low))
    low_2, high_2 = shifted(low_1, 1), shifted(high_3, 3)
    gated_0 = attend_some(full_high, users // 2, gated_low)
    full_1 = [[low, high], [low_1, high_1], [low_2, high_2], [low_3, high_3]]
    gated_1 = attend_packed(
        full_1,
        weight_in,
        history_cache,
        seat_order,
        seat_offsets,
        seat_slots,
        seat_last,
        rank,
        rows_info,
        second_rows,
        heads,
    )
    done_0 = project_out(
        by_quarter(gated_0), (full_low, full_high), weights_out, scalars, 0
    )
    done = project_out_packed(
        by_quarter(gated_1),
        full_1,
        weights_out,
        seat_scalars,
        seat_slots,
        seat_offsets,
        1,
        done_0,
    )

    def unpacked(done, rows):
        every = [rows] + [shifted(rows, k) for k in range(1, mp_size)]
        both = [[r[: users // 2] for r in every], [r[users // 2 :] for r in every]]
        gated = attend_some(both[0], 0)
        gated = by_quarter(attend_some(both[1], users // 2, gated))
        return project_out(gated, both, weights_out, scalars, 1, done)

    done = lax.cond(
        jnp.sum(groups) > SIZE, unpacked, lambda done, rows: done, done, owned_1
    )
    results = lax.all_to_all(
        done.reshape((-1,) + done.shape[2:]), ("dp", "mp"), split_axis=0, concat_axis=0, tiled=True
    )
    return permute_out(place, results.reshape(done.shape))


def solution(mesh):
    in_specs = (
        P("dp", None, "mp"),
        P("dp"),
        P("dp"),
        P(),
        P("dp", None, "mp"),
        P("dp"),
        P(None, "mp"),
        P("mp", None),
        P("mp", None),
    )
    out_specs = P("dp", None, "mp")
    return jax.shard_map(
        per_device, mesh=mesh, in_specs=in_specs, out_specs=out_specs, check_vma=False
    )
```

```python
import math

import jax
import jax.numpy as jnp
from jax import lax
from jax.experimental import pallas as pl
from jax.experimental.pallas import tpu as pltpu
from jax.sharding import PartitionSpec as P

HD = 128
EPSILON = 1e-05
VMEM = 48 * 1024 * 1024

PIECES = ((0, 64), (64, 64))
BATCH = 8
SIZE = 1088
GROUP = 16


def permute_out(index, results):
    users, mp, pieces, quarter, width = results.shape
    rows = pieces * mp * quarter

    def body(index_ref, src, out, buffer, sem):
        def store(i):
            return pltpu.make_async_copy(buffer.at[i], out.at[index_ref[i]], sem.at[i])

        for i in range(users):
            for n in range(pieces):
                for q in range(mp):
                    at = (n * mp + q) * quarter
                    buffer[i, at : at + quarter, :] = src[i, q, n]
            store(i).start()
        for i in range(users):
            store(i).wait()

    return pl.pallas_call(
        body,
        out_shape=jax.ShapeDtypeStruct((users, rows, width), results.dtype),
        in_specs=[
            pl.BlockSpec(memory_space=pltpu.SMEM),
            pl.BlockSpec(memory_space=pltpu.VMEM),
        ],
        out_specs=pl.BlockSpec(memory_space=pl.ANY),
        scratch_shapes=[
            pltpu.VMEM((users, rows, width), results.dtype),
            pltpu.SemaphoreType.DMA((users,)),
        ],
        compiler_params=pltpu.CompilerParams(vmem_limit_bytes=VMEM),
    )(index, results)


def permute_in(index, whole, piece, tags=()):
    users, _, width = whole.shape
    start, size = piece
    rows = size + GROUP if tags else size

    def body(index_ref, *refs):
        src, out = refs[-2:]
        upper = lax.broadcasted_iota(jnp.int32, (GROUP, width), 0) < GROUP // 2
        for i in range(users):
            at = index_ref[i]
            out[i, :size, :] = src[at, start : start + size, :]
            if tags:
                tag = jnp.where(upper, refs[0][at], refs[1][at])
                out[i, size:, :] = tag.astype(jnp.float32).astype(whole.dtype)

    return pl.pallas_call(
        body,
        out_shape=jax.ShapeDtypeStruct((users, rows, width), whole.dtype),
        in_specs=[pl.BlockSpec(memory_space=pltpu.SMEM)] * (1 + len(tags))
        + [pl.BlockSpec(memory_space=pltpu.VMEM)],
        out_specs=pl.BlockSpec(memory_space=pltpu.VMEM),
        compiler_params=pltpu.CompilerParams(vmem_limit_bytes=VMEM),
    )(index, *tags, whole)


def halves(rows, size):
    users, _, width = rows.shape
    half = users // 2

    def body(src, low, high, sem):
        copies = [
            pltpu.make_async_copy(
                src.at[pl.ds(n * half, half), pl.ds(0, size)], (low, high)[n], sem.at[n]
            )
            for n in range(2)
        ]
        for copy in copies:
            copy.start()
        for copy in copies:
            copy.wait()

    return pl.pallas_call(
        body,
        out_shape=[pltpu.HBM((half, size, width), rows.dtype)] * 2,
        in_specs=[pl.BlockSpec(memory_space=pltpu.VMEM)],
        out_specs=[pl.BlockSpec(memory_space=pltpu.HBM)] * 2,
        scratch_shapes=[pltpu.SemaphoreType.DMA((2,))],
        compiler_params=pltpu.CompilerParams(vmem_limit_bytes=VMEM),
    )(rows)


def attend_batch(projected, caches, infos, h, heads):
    inv_scale = 1.0 / math.sqrt(HD)
    batch = len(projected)
    rows = projected[0].shape[0]
    scores = [
        lax.dot_general(
            p[:, 2 * HD : 3 * HD],
            cache[0],
            (((1,), (1,)), ((), ())),
            preferred_element_type=jnp.float32,
        )
        for p, cache in zip(projected, caches)
    ]
    scores = [s * (0.5 * inv_scale) + info[h : h + 1, :] for s, info in zip(scores, infos)]
    weights = [
        ((s + s * jnp.tanh(s)) * info[2 * heads : 2 * heads + 1, :]).astype(jnp.bfloat16)
        for s, info in zip(scores, infos)
    ]
    summed = [
        jnp.dot(w, cache[1], preferred_element_type=jnp.float32)
        for w, cache in zip(weights, caches)
    ]
    whole = jnp.concatenate(projected, axis=0)
    gate, value, query, key = [
        whole[:, k * HD : (k + 1) * HD].astype(jnp.float32) for k in range(4)
    ]
    inverse = jnp.concatenate(
        [
            jnp.broadcast_to(info[2 * heads + 1 : 2 * heads + 2, :HD], (rows, HD))
            for info in infos
        ],
        axis=0,
    )
    own = jnp.sum(query * key, axis=-1, keepdims=True)
    own = own * (0.5 * inv_scale) + infos[0][heads + h : heads + h + 1, :HD]
    own = (own + own * jnp.tanh(own)) * inverse
    own = own.astype(jnp.bfloat16).astype(jnp.float32)
    combined = jnp.concatenate(summed, axis=0) + own * value
    head_mean = jnp.mean(combined, axis=-1, keepdims=True)
    centred = combined - head_mean
    head_var = jnp.mean(centred * centred, axis=-1, keepdims=True)
    return (centred * lax.rsqrt(head_var + EPSILON) * gate).astype(jnp.bfloat16)


def spread_quarters(whole_ref, out_refs, rows, rank):
    mp = len(out_refs)
    quarter = rows // mp
    for k in range(mp):
        at = ((rank + k) % mp) * quarter
        for b in range(BATCH):
            out_refs[k][b] = whole_ref[pl.ds(pl.multiple_of(b * rows + at, GROUP), quarter), :]


def normalise(parts):
    parts = [p.astype(jnp.float32) for p in parts]
    width = len(parts) * parts[0].shape[1]
    mean = sum(jnp.sum(p, axis=-1, keepdims=True) for p in parts) * (1.0 / width)
    parts = [p - mean for p in parts]
    var = sum(jnp.sum(p * p, axis=-1, keepdims=True) for p in parts) * (1.0 / width)
    factor = lax.rsqrt(var + EPSILON)
    return jnp.concatenate([(p * factor).astype(jnp.bfloat16) for p in parts], axis=1)


def silu_dot(normed, weight):
    half = 0.5 * jnp.dot(normed, weight, preferred_element_type=jnp.float32)
    return (half + half * jnp.tanh(half)).astype(jnp.bfloat16)


def head_cache(hist_ref, h):
    return (
        hist_ref[0, :, 2 * h * HD : (2 * h + 1) * HD],
        hist_ref[0, :, (2 * h + 1) * HD : (2 * h + 2) * HD],
    )


def attend(full, weight, history, order, rank, rows_info, heads, first, before):
    mp = len(full)
    some, rows, part = full[0].shape
    users = order.shape[0]
    events, kv_width = history.shape[1:]
    quarter = rows // mp
    total = BATCH * rows
    skip = first // BATCH
    width = heads * HD

    def body(order_ref, rank_ref, *refs):
        full_refs, weight_ref, info_ref = refs[:mp], refs[mp], refs[mp + 1]
        hist_refs = refs[mp + 2 : mp + 2 + BATCH]
        out_refs, store = refs[-1 - mp : -1], refs[-1]
        normed = normalise([f[...].reshape(total, part) for f in full_refs])
        infos = [info_ref.at[b] for b in range(BATCH)]
        for h in range(heads):
            projected = silu_dot(normed, weight_ref[:, h * 4 * HD : (h + 1) * 4 * HD])
            store[:, h * HD : (h + 1) * HD] = attend_batch(
                [projected[b * rows : (b + 1) * rows] for b in range(BATCH)],
                [head_cache(hist_refs[b], h) for b in range(BATCH)],
                infos,
                h,
                heads,
            )
        spread_quarters(store, out_refs, rows, rank_ref[0])

    def hist_spec(b):
        return pl.BlockSpec(
            (1, events, kv_width), lambda i, order, _: (order[(skip + i) * BATCH + b], 0, 0)
        )

    extra = () if before is None else tuple(before)
    inputs = (order, rank, *full, weight, rows_info, *([history] * BATCH), *extra)
    at = len(inputs) - len(extra)
    return pl.pallas_call(
        body,
        out_shape=[pltpu.HBM((users, quarter, width), jnp.bfloat16)] * mp,
        grid_spec=pltpu.PrefetchScalarGridSpec(
            num_scalar_prefetch=2,
            grid=(some // BATCH,),
            in_specs=[pl.BlockSpec((BATCH, rows, part), lambda i, *_: (i, 0, 0)) for _ in full]
            + [
                pl.BlockSpec(weight.shape, lambda i, *_: (0, 0)),
                pl.BlockSpec((BATCH,) + rows_info.shape[1:], lambda i, *_: (skip + i, 0, 0)),
            ]
            + [hist_spec(b) for b in range(BATCH)]
            + [pl.BlockSpec(memory_space=pl.ANY) for _ in extra],
            out_specs=[pl.BlockSpec((BATCH, quarter, width), lambda i, *_: (skip + i, 0, 0))] * mp,
            scratch_shapes=[pltpu.VMEM((total, width), jnp.bfloat16)],
        ),
        input_output_aliases={at + k: k for k in range(len(extra))},
        compiler_params=pltpu.CompilerParams(vmem_limit_bytes=VMEM),
    )(*inputs)


def pack(slots, offsets, rows, size):
    users, count, width = rows.shape
    half = size // 2

    def body(slots_ref, offsets_ref, rows_ref, low, high, buffer, sem):
        for j in range(users):
            at = pl.multiple_of(offsets_ref[j], GROUP)
            buffer[pl.ds(at, count), :] = rows_ref[slots_ref[j]]
        copies = [
            pltpu.make_async_copy(buffer.at[pl.ds(n * half, half)], (low, high)[n], sem.at[n])
            for n in range(2)
        ]
        for copy in copies:
            copy.start()
        for copy in copies:
            copy.wait()

    return pl.pallas_call(
        body,
        out_shape=[pltpu.HBM((half, width), rows.dtype)] * 2,
        in_specs=[
            pl.BlockSpec(memory_space=pltpu.SMEM),
            pl.BlockSpec(memory_space=pltpu.SMEM),
            pl.BlockSpec(memory_space=pltpu.VMEM),
        ],
        out_specs=[pl.BlockSpec(memory_space=pltpu.HBM)] * 2,
        scratch_shapes=[
            pltpu.VMEM((size + count, width), rows.dtype),
            pltpu.SemaphoreType.DMA((2,)),
        ],
        compiler_params=pltpu.CompilerParams(vmem_limit_bytes=VMEM),
    )(slots, offsets, rows)


def attend_packed(
    full, weight, history, order, offsets, seats, last, rank, rows_info, rows, heads
):
    mp = len(full)
    part = full[0][0].shape[1]
    size = sum(array.shape[0] for array in full[0])
    users = order.shape[0]
    events, kv_width = history.shape[1:]
    quarter = rows // mp
    blocks = 4
    block = size // blocks
    count = sum(len(arrays) for arrays in full)

    def body(
        order_ref, offsets_ref, seats_ref, last_ref, rank_ref, *refs
    ):
        weight_ref, info_ref = refs[count], refs[count + 1]
        hist_refs = refs[count + 2 : count + 2 + BATCH]
        out_refs = refs[count + 2 + BATCH : count + 2 + BATCH + mp]
        store, merged = refs[-2:]
        step = pl.program_id(0)

        @pl.when(step < blocks)
        def _():
            parts, at = [], 0
            for arrays in full:
                block_rows = refs[at][...]
                if len(arrays) > 1:
                    low = step < arrays[0].shape[0] // block
                    block_rows = jnp.where(low, block_rows, refs[at + 1][...])
                parts.append(block_rows)
                at = at + len(arrays)
            normed = normalise(parts)
            at = pl.multiple_of(step * block, GROUP)
            store[pl.ds(at, block), :] = silu_dot(normed, weight_ref[...])

        @pl.when((step >= blocks) & (step - blocks <= last_ref[0]))
        def _():
            seats = [(step - blocks) * BATCH + b for b in range(BATCH)]
            starts = [pl.multiple_of(offsets_ref[j], GROUP) for j in seats]
            infos = [info_ref.at[seats_ref[j]] for j in seats]
            for h in range(heads):
                merged[:, h * HD : (h + 1) * HD] = attend_batch(
                    [store[pl.ds(at, rows), h * 4 * HD : (h + 1) * 4 * HD] for at in starts],
                    [head_cache(hist_refs[b], h) for b in range(BATCH)],
                    infos,
                    h,
                    heads,
                )
            spread_quarters(merged, out_refs, rows, rank_ref[0])

    def full_spec(array, n):
        steps = array.shape[0] // block
        return pl.BlockSpec((block, part), lambda i, *_: (jnp.clip(i - n * steps, 0, steps - 1), 0))

    def batch_of(i):
        return jnp.maximum(i - blocks, 0)

    def hist_spec(b):
        return pl.BlockSpec(
            (1, events, kv_width),
            lambda i, order, offsets, seats, last, rank: (
                order[jnp.minimum(batch_of(i), last[0]) * BATCH + b],
                0,
                0,
            ),
        )

    width = heads * HD
    return pl.pallas_call(
        body,
        out_shape=[pltpu.HBM((users, quarter, width), jnp.bfloat16)] * mp,
        grid_spec=pltpu.PrefetchScalarGridSpec(
            num_scalar_prefetch=5,
            grid=(blocks + users // BATCH,),
            in_specs=[full_spec(array, n) for arrays in full for n, array in enumerate(arrays)]
            + [
                pl.BlockSpec(weight.shape, lambda i, *_: (0, 0)),
                pl.BlockSpec(rows_info.shape, lambda i, *_: (0, 0, 0)),
            ]
            + [hist_spec(b) for b in range(BATCH)],
            out_specs=[pl.BlockSpec((BATCH, quarter, width), lambda i, *_: (batch_of(i), 0, 0))]
            * mp,
            scratch_shapes=[
                pltpu.VMEM((size + rows, weight.shape[1]), jnp.bfloat16),
                pltpu.VMEM((BATCH * rows, width), jnp.bfloat16),
            ],
        ),
        compiler_params=pltpu.CompilerParams(vmem_limit_bytes=VMEM),
    )(order, offsets, seats, last, rank, *sum(full, []), weight, rows_info, *([history] * BATCH))


def rank_dot(gated, weights):
    terms = [
        jnp.dot(g, w, preferred_element_type=jnp.float32) for g, w in zip(gated, weights)
    ]
    return sum(terms[1:], terms[0])


def project_out(gated, full, weights, scalars, piece, before=None):
    mp = len(gated)
    users, quarter, part = gated[0].shape
    out_part = weights[0].shape[1] // mp
    batch = 8
    per_half = users // 2 // batch
    start = PIECES[piece][0]
    extra = () if before is None else (before,)

    def body(scalar_ref, *refs):
        full_refs, gated_refs = refs[: 2 * mp], refs[2 * mp : 3 * mp]
        weight_refs, out_ref = refs[3 * mp : 4 * mp], refs[-1]
        step = pl.program_id(0)
        rank = scalar_ref[0]
        rows = [g[...].reshape(batch * quarter, part) for g in gated_refs]
        row = lax.broadcasted_iota(jnp.int32, (quarter, out_part), 0) + (start + rank * quarter)
        for k in range(mp):
            column = (rank + (mp - k)) % mp
            at = pl.multiple_of(column * out_part, out_part)
            acc = rank_dot(rows, [w[:, pl.ds(at, out_part)] for w in weight_refs])
            for b in range(batch):
                alive = row < scalar_ref[1 + step * batch + b]
                residual = jnp.where(step < per_half, full_refs[k][b], full_refs[mp + k][b])
                mine = acc[b * quarter : (b + 1) * quarter] + residual.astype(jnp.float32)
                out_ref[b, column, 0] = jnp.where(alive, mine, 0.0).astype(jnp.bfloat16)

    def full_spec(n):
        return pl.BlockSpec(
            (batch, quarter, part),
            lambda i, s: (jnp.clip(i - n * per_half, 0, per_half - 1), s[0], 0),
        )

    return pl.pallas_call(
        body,
        out_shape=jax.ShapeDtypeStruct((users, mp, len(PIECES), quarter, out_part), jnp.bfloat16),
        grid_spec=pltpu.PrefetchScalarGridSpec(
            num_scalar_prefetch=1,
            grid=(users // batch,),
            in_specs=[full_spec(n) for n in range(2) for _ in range(mp)]
            + [pl.BlockSpec((batch, quarter, part), lambda i, s: (i, 0, 0)) for _ in gated]
            + [pl.BlockSpec(w.shape, lambda i, s: (0, 0)) for w in weights]
            + [pl.BlockSpec(memory_space=pl.ANY) for _ in extra],
            out_specs=pl.BlockSpec(
                (batch, mp, 1, quarter, out_part), lambda i, s: (i, 0, piece, 0, 0)
            ),
        ),
        input_output_aliases={1 + 4 * mp: 0} if extra else {},
        compiler_params=pltpu.CompilerParams(vmem_limit_bytes=VMEM),
    )(scalars, *full[0], *full[1], *gated, *weights, *extra)


def project_out_packed(gated, full, weights, scalars, slots, offsets, piece, before):
    mp = len(gated)
    users, quarter, part = gated[0].shape
    half = full[0][0].shape[0]
    out_part = weights[0].shape[1] // mp
    start = PIECES[piece][0]

    def body(scalar_ref, slots_ref, offsets_ref, *refs):
        full_refs, gated_refs = refs[: 2 * mp], refs[2 * mp : 3 * mp]
        weight_refs = refs[3 * mp : 4 * mp]
        out_ref, whole, store, sem = refs[-4:]
        rank = scalar_ref[0]
        rows = [g[...].reshape(users * quarter, part) for g in gated_refs]
        row = lax.broadcasted_iota(jnp.int32, (quarter, out_part), 0) + (start + rank * quarter)

        def copy(k):
            column = (rank + (mp - k)) % mp
            return pltpu.make_async_copy(store.at[k], out_ref.at[:, column, piece], sem.at[k])

        for k in range(mp):
            whole[:half, :] = full_refs[2 * k][...]
            whole[half:, :] = full_refs[2 * k + 1][...]
            column = (rank + (mp - k)) % mp
            first = pl.multiple_of(column * out_part, out_part)
            acc = rank_dot(rows, [w[:, pl.ds(first, out_part)] for w in weight_refs])
            for j in range(users):
                at = jnp.minimum(offsets_ref[j] + rank * quarter, 2 * half - quarter)
                residual = whole[pl.ds(pl.multiple_of(at, GROUP), quarter), :]
                mine = acc[j * quarter : (j + 1) * quarter] + residual.astype(jnp.float32)
                alive = row < scalar_ref[1 + j]
                store[k, slots_ref[j]] = jnp.where(alive, mine, 0.0).astype(jnp.bfloat16)
            copy(k).start()
        for k in range(mp):
            copy(k).wait()

    arrays = [array for arrays in full for array in arrays]
    return pl.pallas_call(
        body,
        out_shape=jax.ShapeDtypeStruct((users, mp, len(PIECES), quarter, out_part), jnp.bfloat16),
        in_specs=[pl.BlockSpec(memory_space=pltpu.SMEM)] * 3
        + [pl.BlockSpec(memory_space=pltpu.VMEM)] * (4 * mp)
        + [pl.BlockSpec(memory_space=pl.ANY)],
        out_specs=pl.BlockSpec(memory_space=pl.ANY),
        scratch_shapes=[
            pltpu.VMEM((2 * half, part), jnp.bfloat16),
            pltpu.VMEM((mp, users, quarter, out_part), jnp.bfloat16),
            pltpu.SemaphoreType.DMA((mp,)),
        ],
        input_output_aliases={3 + 4 * mp: 0},
        compiler_params=pltpu.CompilerParams(vmem_limit_bytes=VMEM),
    )(scalars, slots, offsets, *arrays, *gated, *weights, before)


def bucket_bias(distance, time_bias):
    bias = jnp.broadcast_to(time_bias[:, 0][:, None, None], time_bias.shape[:1] + distance.shape)
    for k in range(time_bias.shape[1] - 1):
        bias = jnp.where((distance >= 2**k)[None], time_bias[:, k + 1][:, None, None], bias)
    return bias


def per_device(
    candidates,
    live_counts,
    request_user,
    score_slot,
    history_cache,
    history_length,
    input_weight,
    time_bias,
    output_weight,
):
    dp_size = lax.axis_size("dp")
    dp_rank = lax.axis_index("dp")
    mp_rank = lax.axis_index("mp")
    users, slots, part = candidates.shape
    events = history_cache.shape[1]
    heads = time_bias.shape[0]
    ranks = jnp.arange(dp_size, dtype=jnp.int32)
    local = jnp.arange(users, dtype=jnp.int32)
    scorer = score_slot // users

    target = jnp.take(scorer, request_user)
    send_first = jnp.sum(jnp.where(target[None, :] == ranks[:, None], local[None, :], 0), axis=1)
    def exchange(rows):
        return lax.all_to_all(rows, "dp", split_axis=0, concat_axis=0, tiled=True)

    mp_size = lax.axis_size("mp")

    def shifted(array, k):
        return lax.ppermute(array, "mp", [(i, (i + k) % mp_size) for i in range(mp_size)])

    first_rows, second_rows = PIECES[0][1], PIECES[1][1]
    weights_out = [output_weight] + [shifted(output_weight, k) for k in range(1, mp_size)]
    rows_0 = permute_in(send_first, candidates, PIECES[0], (request_user // users, live_counts))
    scored_0 = exchange(rows_0)
    owner_rank = scored_0[:, first_rows, 0].astype(jnp.int32)
    send_second = jnp.sum(
        jnp.where(owner_rank[None, :] == ranks[:, None], ranks[None, :], 0), axis=1
    )
    tagged_0 = exchange(permute_in(send_second, scored_0, (0, first_rows + GROUP)))
    owned_0 = halves(tagged_0, first_rows)
    live = tagged_0[:, first_rows + GROUP // 2, 0].astype(jnp.int32)

    scored_here = scorer.reshape(dp_size, users) == dp_rank
    place = jnp.sum(
        jnp.where(scored_here, score_slot.reshape(dp_size, users), 0), axis=1
    ) - dp_rank * users
    own_scorer = lax.dynamic_slice_in_dim(scorer, dp_rank * users, users)
    order = jnp.sum(jnp.where(own_scorer[None, :] == ranks[:, None], local[None, :], 0), axis=1)
    scalars = jnp.concatenate([mp_rank[None], live]).astype(jnp.int32)

    lengths = jnp.take(history_length, order)
    position = jnp.arange(events, dtype=jnp.int32)
    distance = lengths[:, None] - position[None, :]
    inverse = 1.0 / (lengths + 1).astype(jnp.float32)
    spread = jnp.broadcast_to(inverse[:, None], (users, events))
    bias = 0.5 * bucket_bias(distance, time_bias)
    own_bias = jnp.broadcast_to(0.5 * time_bias[:, 0][:, None, None], bias.shape)
    info = [bias[h] for h in range(heads)] + [own_bias[h] for h in range(heads)]
    info = info + [jnp.where(distance > 0, spread, 0.0), spread]
    info = info + [jnp.zeros_like(spread)] * (-len(info) % 8)
    rows_info = jnp.stack(info, axis=1)

    def padded(count):
        return (jnp.maximum(count - first_rows, 0) + (GROUP - 1)) // GROUP * GROUP

    groups = padded(live)
    has = groups > 0
    earlier = local[None, :] < local[:, None]
    count = jnp.sum(has.astype(jnp.int32))
    seat = jnp.where(
        has,
        jnp.sum((earlier & has[None, :]).astype(jnp.int32), axis=1),
        count + jnp.sum((earlier & ~has[None, :]).astype(jnp.int32), axis=1),
    )
    seated = seat[None, :] == local[:, None]

    def by_seat(values):
        return jnp.sum(jnp.where(seated, values[None, :], 0), axis=1).astype(jnp.int32)

    seat_slots = by_seat(local)
    seat_order = by_seat(order)
    seat_scalars = jnp.concatenate([mp_rank[None], by_seat(live)]).astype(jnp.int32)
    seat_offsets = jnp.sum(
        jnp.where(seat[None, :] < local[:, None], groups[None, :], 0), axis=1
    ).astype(jnp.int32)
    seat_offsets = jnp.minimum(seat_offsets, SIZE)
    rank = mp_rank[None].astype(jnp.int32)
    seat_last = (jnp.maximum(count - 1, 0) // BATCH)[None].astype(jnp.int32)

    turned = (mp_rank + (mp_size - jnp.arange(mp_size, dtype=jnp.int32))) % mp_size
    weight_in = jnp.take(input_weight.reshape(mp_size, part, -1), turned, axis=0)
    weight_in = weight_in.reshape(input_weight.shape)

    def by_quarter(gated):
        return [gated[0]] + [shifted(gated[k], k) for k in range(1, mp_size)]

    rows_1 = permute_in(send_first, candidates, PIECES[1])
    rows_1, owned_0, rows_info, weight_in, *weights_out = lax.optimization_barrier(
        (rows_1, owned_0, rows_info, weight_in, *weights_out)
    )
    low_0, high_0 = owned_0
    full_low = [low_0, shifted(low_0, 1), None, shifted(low_0, 3)]
    full_low[2] = shifted(full_low[1], 1)
    full_high = [high_0, shifted(high_0, 1), None, shifted(high_0, 3)]
    full_high[2] = shifted(full_high[3], 3)
    owned_1 = exchange(permute_in(send_second, exchange(rows_1), (0, second_rows)))
    owned_1, groups = lax.optimization_barrier((owned_1, groups))
    packed = pack(seat_slots, seat_offsets, owned_1, SIZE)
    low, high = packed

    def attend_some(full, first, before=None):
        return attend(
            full, weight_in, history_cache, order, rank, rows_info, heads, first, before
        )

    gated_low = attend_some(full_low, 0)
    low_1, high_3 = shifted(low, 1), shifted(high, 3)
    high_1, low_3 = shifted(high, 1), shifted(low, 3)
    low_1, high_3, gated_low = lax.optimization_barrier((low_1, high_3, gated_low))
    low_2, high_2 = shifted(low_1, 1), shifted(high_3, 3)
    gated_0 = attend_some(full_high, users // 2, gated_low)
    full_1 = [[low, high], [low_1, high_1], [low_2, high_2], [low_3, high_3]]
    gated_1 = attend_packed(
        full_1,
        weight_in,
        history_cache,
        seat_order,
        seat_offsets,
        seat_slots,
        seat_last,
        rank,
        rows_info,
        second_rows,
        heads,
    )
    done_0 = project_out(
        by_quarter(gated_0), (full_low, full_high), weights_out, scalars, 0
    )
    done = project_out_packed(
        by_quarter(gated_1),
        full_1,
        weights_out,
        seat_scalars,
        seat_slots,
        seat_offsets,
        1,
        done_0,
    )

    def unpacked(done, rows):
        every = [rows] + [shifted(rows, k) for k in range(1, mp_size)]
        both = [[r[: users // 2] for r in every], [r[users // 2 :] for r in every]]
        gated = attend_some(both[0], 0)
        gated = by_quarter(attend_some(both[1], users // 2, gated))
        return project_out(gated, both, weights_out, scalars, 1, done)

    done = lax.cond(
        jnp.sum(groups) > SIZE, unpacked, lambda done, rows: done, done, owned_1
    )
    results = lax.all_to_all(
        done.reshape((-1,) + done.shape[2:]), ("dp", "mp"), split_axis=0, concat_axis=0, tiled=True
    )
    return permute_out(place, results.reshape(done.shape))


def solution(mesh):
    in_specs = (
        P("dp", None, "mp"),
        P("dp"),
        P("dp"),
        P(),
        P("dp", None, "mp"),
        P("dp"),
        P(None, "mp"),
        P("mp", None),
        P("mp", None),
    )
    out_specs = P("dp", None, "mp")
    return jax.shard_map(
        per_device, mesh=mesh, in_specs=in_specs, out_specs=out_specs, check_vma=False
    )
```

```python
import math

import jax
import jax.numpy as jnp
from jax import lax
from jax.experimental import pallas as pl
from jax.experimental.pallas import tpu as pltpu
from jax.sharding import PartitionSpec as P

HD = 128
EPSILON = 1e-05
VMEM = 48 * 1024 * 1024

PIECES = ((0, 64), (64, 64))
BATCH = 8
SIZE = 1088
GROUP = 16


def permute_out(index, results):
    users, mp, pieces, quarter, width = results.shape
    rows = pieces * mp * quarter

    def body(index_ref, src, out, buffer, sem):
        def store(i):
            return pltpu.make_async_copy(buffer.at[i], out.at[index_ref[i]], sem.at[i])

        for i in range(users):
            for n in range(pieces):
                for q in range(mp):
                    at = (n * mp + q) * quarter
                    buffer[i, at : at + quarter, :] = src[i, q, n]
            store(i).start()
        for i in range(users):
            store(i).wait()

    return pl.pallas_call(
        body,
        out_shape=jax.ShapeDtypeStruct((users, rows, width), results.dtype),
        in_specs=[
            pl.BlockSpec(memory_space=pltpu.SMEM),
            pl.BlockSpec(memory_space=pltpu.VMEM),
        ],
        out_specs=pl.BlockSpec(memory_space=pl.ANY),
        scratch_shapes=[
            pltpu.VMEM((users, rows, width), results.dtype),
            pltpu.SemaphoreType.DMA((users,)),
        ],
        compiler_params=pltpu.CompilerParams(vmem_limit_bytes=VMEM),
    )(index, results)


def permute_in(index, whole, piece, tags=()):
    users, _, width = whole.shape
    start, size = piece
    rows = size + GROUP if tags else size

    def body(index_ref, *refs):
        src, out = refs[-2:]
        upper = lax.broadcasted_iota(jnp.int32, (GROUP, width), 0) < GROUP // 2
        for i in range(users):
            at = index_ref[i]
            out[i, :size, :] = src[at, start : start + size, :]
            if tags:
                tag = jnp.where(upper, refs[0][at], refs[1][at])
                out[i, size:, :] = tag.astype(jnp.float32).astype(whole.dtype)

    return pl.pallas_call(
        body,
        out_shape=jax.ShapeDtypeStruct((users, rows, width), whole.dtype),
        in_specs=[pl.BlockSpec(memory_space=pltpu.SMEM)] * (1 + len(tags))
        + [pl.BlockSpec(memory_space=pltpu.VMEM)],
        out_specs=pl.BlockSpec(memory_space=pltpu.VMEM),
        compiler_params=pltpu.CompilerParams(vmem_limit_bytes=VMEM),
    )(index, *tags, whole)


def halves(rows, size):
    users, _, width = rows.shape
    half = users // 2

    def body(src, low, high, sem):
        copies = [
            pltpu.make_async_copy(
                src.at[pl.ds(n * half, half), pl.ds(0, size)], (low, high)[n], sem.at[n]
            )
            for n in range(2)
        ]
        for copy in copies:
            copy.start()
        for copy in copies:
            copy.wait()

    return pl.pallas_call(
        body,
        out_shape=[pltpu.HBM((half, size, width), rows.dtype)] * 2,
        in_specs=[pl.BlockSpec(memory_space=pltpu.VMEM)],
        out_specs=[pl.BlockSpec(memory_space=pltpu.HBM)] * 2,
        scratch_shapes=[pltpu.SemaphoreType.DMA((2,))],
        compiler_params=pltpu.CompilerParams(vmem_limit_bytes=VMEM),
    )(rows)


def attend_batch(projected, caches, infos, h, heads):
    inv_scale = 1.0 / math.sqrt(HD)
    batch = len(projected)
    rows = projected[0].shape[0]
    scores = [
        lax.dot_general(
            p[:, 2 * HD : 3 * HD],
            cache[0],
            (((1,), (1,)), ((), ())),
            preferred_element_type=jnp.float32,
        )
        for p, cache in zip(projected, caches)
    ]
    scores = [s * (0.5 * inv_scale) + info[h : h + 1, :] for s, info in zip(scores, infos)]
    weights = [
        ((s + s * jnp.tanh(s)) * info[2 * heads : 2 * heads + 1, :]).astype(jnp.bfloat16)
        for s, info in zip(scores, infos)
    ]
    summed = [
        jnp.dot(w, cache[1], preferred_element_type=jnp.float32)
        for w, cache in zip(weights, caches)
    ]
    whole = jnp.concatenate(projected, axis=0)
    gate, value, query, key = [
        whole[:, k * HD : (k + 1) * HD].astype(jnp.float32) for k in range(4)
    ]
    inverse = jnp.concatenate(
        [
            jnp.broadcast_to(info[2 * heads + 1 : 2 * heads + 2, :HD], (rows, HD))
            for info in infos
        ],
        axis=0,
    )
    own = jnp.sum(query * key, axis=-1, keepdims=True)
    own = own * (0.5 * inv_scale) + infos[0][heads + h : heads + h + 1, :HD]
    own = (own + own * jnp.tanh(own)) * inverse
    own = own.astype(jnp.bfloat16).astype(jnp.float32)
    combined = jnp.concatenate(summed, axis=0) + own * value
    head_mean = jnp.mean(combined, axis=-1, keepdims=True)
    centred = combined - head_mean
    head_var = jnp.mean(centred * centred, axis=-1, keepdims=True)
    return (centred * lax.rsqrt(head_var + EPSILON) * gate).astype(jnp.bfloat16)


def spread_quarters(whole_ref, out_refs, rows, rank):
    mp = len(out_refs)
    quarter = rows // mp
    for k in range(mp):
        at = ((rank + k) % mp) * quarter
        for b in range(BATCH):
            out_refs[k][b] = whole_ref[pl.ds(pl.multiple_of(b * rows + at, GROUP), quarter), :]


def normalise(parts):
    parts = [p.astype(jnp.float32) for p in parts]
    width = len(parts) * parts[0].shape[1]
    mean = sum(jnp.sum(p, axis=-1, keepdims=True) for p in parts) * (1.0 / width)
    parts = [p - mean for p in parts]
    var = sum(jnp.sum(p * p, axis=-1, keepdims=True) for p in parts) * (1.0 / width)
    factor = lax.rsqrt(var + EPSILON)
    return jnp.concatenate([(p * factor).astype(jnp.bfloat16) for p in parts], axis=1)


def silu_dot(normed, weight):
    half = 0.5 * jnp.dot(normed, weight, preferred_element_type=jnp.float32)
    return (half + half * jnp.tanh(half)).astype(jnp.bfloat16)


def head_cache(hist_ref, h):
    return (
        hist_ref[0, :, 2 * h * HD : (2 * h + 1) * HD],
        hist_ref[0, :, (2 * h + 1) * HD : (2 * h + 2) * HD],
    )


def attend(full, weight, history, order, rank, rows_info, heads):
    mp = len(full[0])
    half, rows, part = full[0][0].shape
    users = order.shape[0]
    events, kv_width = history.shape[1:]
    quarter = rows // mp
    total = BATCH * rows
    width = heads * HD
    per_half = half // BATCH

    def body(order_ref, rank_ref, *refs):
        full_refs, weight_ref, info_ref = refs[: 2 * mp], refs[2 * mp], refs[2 * mp + 1]
        hist_refs = refs[2 * mp + 2 : 2 * mp + 2 + BATCH]
        out_refs, store = refs[-1 - mp : -1], refs[-1]
        low = pl.program_id(0) < per_half
        parts = [jnp.where(low, full_refs[k][...], full_refs[mp + k][...]) for k in range(mp)]
        normed = normalise([p.reshape(total, part) for p in parts])
        infos = [info_ref.at[b] for b in range(BATCH)]
        for h in range(heads):
            projected = silu_dot(normed, weight_ref[:, h * 4 * HD : (h + 1) * 4 * HD])
            store[:, h * HD : (h + 1) * HD] = attend_batch(
                [projected[b * rows : (b + 1) * rows] for b in range(BATCH)],
                [head_cache(hist_refs[b], h) for b in range(BATCH)],
                infos,
                h,
                heads,
            )
        spread_quarters(store, out_refs, rows, rank_ref[0])

    def full_spec(n):
        return pl.BlockSpec(
            (BATCH, rows, part), lambda i, *_: (jnp.clip(i - n * per_half, 0, per_half - 1), 0, 0)
        )

    def hist_spec(b):
        return pl.BlockSpec((1, events, kv_width), lambda i, order, _: (order[i * BATCH + b], 0, 0))

    return pl.pallas_call(
        body,
        out_shape=[pltpu.HBM((users, quarter, width), jnp.bfloat16)] * mp,
        grid_spec=pltpu.PrefetchScalarGridSpec(
            num_scalar_prefetch=2,
            grid=(users // BATCH,),
            in_specs=[full_spec(n) for n in range(2) for _ in range(mp)]
            + [
                pl.BlockSpec(weight.shape, lambda i, *_: (0, 0)),
                pl.BlockSpec((BATCH,) + rows_info.shape[1:], lambda i, *_: (i, 0, 0)),
            ]
            + [hist_spec(b) for b in range(BATCH)],
            out_specs=[pl.BlockSpec((BATCH, quarter, width), lambda i, *_: (i, 0, 0))] * mp,
            scratch_shapes=[pltpu.VMEM((total, width), jnp.bfloat16)],
        ),
        compiler_params=pltpu.CompilerParams(vmem_limit_bytes=VMEM),
    )(order, rank, *full[0], *full[1], weight, rows_info, *([history] * BATCH))


def pack(slots, offsets, rows, size):
    users, count, width = rows.shape

    def body(slots_ref, offsets_ref, rows_ref, out, buffer, sem):
        for j in range(users):
            at = pl.multiple_of(offsets_ref[j], GROUP)
            buffer[pl.ds(at, count), :] = rows_ref[slots_ref[j]]
        copy = pltpu.make_async_copy(buffer.at[pl.ds(0, size)], out, sem)
        copy.start()
        copy.wait()

    return pl.pallas_call(
        body,
        out_shape=pltpu.HBM((size, width), rows.dtype),
        in_specs=[
            pl.BlockSpec(memory_space=pltpu.SMEM),
            pl.BlockSpec(memory_space=pltpu.SMEM),
            pl.BlockSpec(memory_space=pltpu.VMEM),
        ],
        out_specs=pl.BlockSpec(memory_space=pltpu.HBM),
        scratch_shapes=[
            pltpu.VMEM((size + count, width), rows.dtype),
            pltpu.SemaphoreType.DMA,
        ],
        compiler_params=pltpu.CompilerParams(vmem_limit_bytes=VMEM),
    )(slots, offsets, rows)


def attend_packed(
    full, weight, history, order, offsets, seats, last, rank, rows_info, rows, heads
):
    mp = len(full)
    part = full[0][0].shape[1]
    size = sum(array.shape[0] for array in full[0])
    users = order.shape[0]
    events, kv_width = history.shape[1:]
    quarter = rows // mp
    blocks = 4
    block = size // blocks
    count = sum(len(arrays) for arrays in full)

    def body(
        order_ref, offsets_ref, seats_ref, last_ref, rank_ref, *refs
    ):
        weight_ref, info_ref = refs[count], refs[count + 1]
        hist_refs = refs[count + 2 : count + 2 + BATCH]
        out_refs = refs[count + 2 + BATCH : count + 2 + BATCH + mp]
        store, merged = refs[-2:]
        step = pl.program_id(0)

        @pl.when(step < blocks)
        def _():
            parts, at = [], 0
            for arrays in full:
                block_rows = refs[at][...]
                if len(arrays) > 1:
                    low = step < arrays[0].shape[0] // block
                    block_rows = jnp.where(low, block_rows, refs[at + 1][...])
                parts.append(block_rows)
                at = at + len(arrays)
            normed = normalise(parts)
            at = pl.multiple_of(step * block, GROUP)
            store[pl.ds(at, block), :] = silu_dot(normed, weight_ref[...])

        @pl.when((step >= blocks) & (step - blocks <= last_ref[0]))
        def _():
            seats = [(step - blocks) * BATCH + b for b in range(BATCH)]
            starts = [pl.multiple_of(offsets_ref[j], GROUP) for j in seats]
            infos = [info_ref.at[seats_ref[j]] for j in seats]
            for h in range(heads):
                merged[:, h * HD : (h + 1) * HD] = attend_batch(
                    [store[pl.ds(at, rows), h * 4 * HD : (h + 1) * 4 * HD] for at in starts],
                    [head_cache(hist_refs[b], h) for b in range(BATCH)],
                    infos,
                    h,
                    heads,
                )
            spread_quarters(merged, out_refs, rows, rank_ref[0])

    def full_spec(array, n):
        steps = array.shape[0] // block
        return pl.BlockSpec((block, part), lambda i, *_: (jnp.clip(i - n * steps, 0, steps - 1), 0))

    def batch_of(i):
        return jnp.maximum(i - blocks, 0)

    def hist_spec(b):
        return pl.BlockSpec(
            (1, events, kv_width),
            lambda i, order, offsets, seats, last, rank: (
                order[jnp.minimum(batch_of(i), last[0]) * BATCH + b],
                0,
                0,
            ),
        )

    width = heads * HD
    return pl.pallas_call(
        body,
        out_shape=[pltpu.HBM((users, quarter, width), jnp.bfloat16)] * mp,
        grid_spec=pltpu.PrefetchScalarGridSpec(
            num_scalar_prefetch=5,
            grid=(blocks + users // BATCH,),
            in_specs=[full_spec(array, n) for arrays in full for n, array in enumerate(arrays)]
            + [
                pl.BlockSpec(weight.shape, lambda i, *_: (0, 0)),
                pl.BlockSpec(rows_info.shape, lambda i, *_: (0, 0, 0)),
            ]
            + [hist_spec(b) for b in range(BATCH)],
            out_specs=[pl.BlockSpec((BATCH, quarter, width), lambda i, *_: (batch_of(i), 0, 0))]
            * mp,
            scratch_shapes=[
                pltpu.VMEM((size + rows, weight.shape[1]), jnp.bfloat16),
                pltpu.VMEM((BATCH * rows, width), jnp.bfloat16),
            ],
        ),
        compiler_params=pltpu.CompilerParams(vmem_limit_bytes=VMEM),
    )(order, offsets, seats, last, rank, *sum(full, []), weight, rows_info, *([history] * BATCH))


def rank_dot(gated, weights):
    terms = [
        jnp.dot(g, w, preferred_element_type=jnp.float32) for g, w in zip(gated, weights)
    ]
    return sum(terms[1:], terms[0])


def project_out(gated, full, weights, scalars, piece, before=None):
    mp = len(gated)
    users, quarter, part = gated[0].shape
    out_part = weights[0].shape[1] // mp
    batch = 8
    per_half = users // 2 // batch
    start = PIECES[piece][0]
    extra = () if before is None else (before,)

    def body(scalar_ref, *refs):
        full_refs, gated_refs = refs[: 2 * mp], refs[2 * mp : 3 * mp]
        weight_refs, out_ref = refs[3 * mp : 4 * mp], refs[-1]
        step = pl.program_id(0)
        rank = scalar_ref[0]
        rows = [g[...].reshape(batch * quarter, part) for g in gated_refs]
        row = lax.broadcasted_iota(jnp.int32, (quarter, out_part), 0) + (start + rank * quarter)
        for k in range(mp):
            column = (rank + (mp - k)) % mp
            at = pl.multiple_of(column * out_part, out_part)
            acc = rank_dot(rows, [w[:, pl.ds(at, out_part)] for w in weight_refs])
            for b in range(batch):
                alive = row < scalar_ref[1 + step * batch + b]
                residual = jnp.where(step < per_half, full_refs[k][b], full_refs[mp + k][b])
                mine = acc[b * quarter : (b + 1) * quarter] + residual.astype(jnp.float32)
                out_ref[b, column, 0] = jnp.where(alive, mine, 0.0).astype(jnp.bfloat16)

    def full_spec(n):
        return pl.BlockSpec(
            (batch, quarter, part),
            lambda i, s: (jnp.clip(i - n * per_half, 0, per_half - 1), s[0], 0),
        )

    return pl.pallas_call(
        body,
        out_shape=jax.ShapeDtypeStruct((users, mp, len(PIECES), quarter, out_part), jnp.bfloat16),
        grid_spec=pltpu.PrefetchScalarGridSpec(
            num_scalar_prefetch=1,
            grid=(users // batch,),
            in_specs=[full_spec(n) for n in range(2) for _ in range(mp)]
            + [pl.BlockSpec((batch, quarter, part), lambda i, s: (i, 0, 0)) for _ in gated]
            + [pl.BlockSpec(w.shape, lambda i, s: (0, 0)) for w in weights]
            + [pl.BlockSpec(memory_space=pl.ANY) for _ in extra],
            out_specs=pl.BlockSpec(
                (batch, mp, 1, quarter, out_part), lambda i, s: (i, 0, piece, 0, 0)
            ),
        ),
        input_output_aliases={1 + 4 * mp: 0} if extra else {},
        compiler_params=pltpu.CompilerParams(vmem_limit_bytes=VMEM),
    )(scalars, *full[0], *full[1], *gated, *weights, *extra)


def project_out_packed(gated, full, weights, scalars, slots, offsets, piece, before):
    mp = len(gated)
    users, quarter, part = gated[0].shape
    size = full[0][0].shape[0]
    out_part = weights[0].shape[1] // mp
    start = PIECES[piece][0]

    def body(scalar_ref, slots_ref, offsets_ref, *refs):
        full_refs, gated_refs = refs[:mp], refs[mp : 2 * mp]
        weight_refs = refs[2 * mp : 3 * mp]
        out_ref, store, sem = refs[-3:]
        rank = scalar_ref[0]
        rows = [g[...].reshape(users * quarter, part) for g in gated_refs]
        row = lax.broadcasted_iota(jnp.int32, (quarter, out_part), 0) + (start + rank * quarter)

        def copy(k):
            column = (rank + (mp - k)) % mp
            return pltpu.make_async_copy(store.at[k], out_ref.at[:, column, piece], sem.at[k])

        for k in range(mp):
            column = (rank + (mp - k)) % mp
            first = pl.multiple_of(column * out_part, out_part)
            acc = rank_dot(rows, [w[:, pl.ds(first, out_part)] for w in weight_refs])
            for j in range(users):
                at = jnp.minimum(offsets_ref[j] + rank * quarter, size - quarter)
                residual = full_refs[k][pl.ds(pl.multiple_of(at, GROUP), quarter), :]
                mine = acc[j * quarter : (j + 1) * quarter] + residual.astype(jnp.float32)
                alive = row < scalar_ref[1 + j]
                store[k, slots_ref[j]] = jnp.where(alive, mine, 0.0).astype(jnp.bfloat16)
            copy(k).start()
        for k in range(mp):
            copy(k).wait()

    arrays = [array for arrays in full for array in arrays]
    return pl.pallas_call(
        body,
        out_shape=jax.ShapeDtypeStruct((users, mp, len(PIECES), quarter, out_part), jnp.bfloat16),
        in_specs=[pl.BlockSpec(memory_space=pltpu.SMEM)] * 3
        + [pl.BlockSpec(memory_space=pltpu.VMEM)] * (3 * mp)
        + [pl.BlockSpec(memory_space=pl.ANY)],
        out_specs=pl.BlockSpec(memory_space=pl.ANY),
        scratch_shapes=[
            pltpu.VMEM((mp, users, quarter, out_part), jnp.bfloat16),
            pltpu.SemaphoreType.DMA((mp,)),
        ],
        input_output_aliases={3 + 3 * mp: 0},
        compiler_params=pltpu.CompilerParams(vmem_limit_bytes=VMEM),
    )(scalars, slots, offsets, *arrays, *gated, *weights, before)


def bucket_bias(distance, time_bias):
    bias = jnp.broadcast_to(time_bias[:, 0][:, None, None], time_bias.shape[:1] + distance.shape)
    for k in range(time_bias.shape[1] - 1):
        bias = jnp.where((distance >= 2**k)[None], time_bias[:, k + 1][:, None, None], bias)
    return bias


def per_device(
    candidates,
    live_counts,
    request_user,
    score_slot,
    history_cache,
    history_length,
    input_weight,
    time_bias,
    output_weight,
):
    dp_size = lax.axis_size("dp")
    dp_rank = lax.axis_index("dp")
    mp_rank = lax.axis_index("mp")
    users, slots, part = candidates.shape
    events = history_cache.shape[1]
    heads = time_bias.shape[0]
    ranks = jnp.arange(dp_size, dtype=jnp.int32)
    local = jnp.arange(users, dtype=jnp.int32)
    scorer = score_slot // users

    target = jnp.take(scorer, request_user)
    send_first = jnp.sum(jnp.where(target[None, :] == ranks[:, None], local[None, :], 0), axis=1)
    def exchange(rows):
        return lax.all_to_all(rows, "dp", split_axis=0, concat_axis=0, tiled=True)

    mp_size = lax.axis_size("mp")

    def shifted(array, k):
        return lax.ppermute(array, "mp", [(i, (i + k) % mp_size) for i in range(mp_size)])

    first_rows, second_rows = PIECES[0][1], PIECES[1][1]
    weights_out = [output_weight] + [shifted(output_weight, k) for k in range(1, mp_size)]
    rows_0 = permute_in(send_first, candidates, PIECES[0], (request_user // users, live_counts))
    scored_0 = exchange(rows_0)
    owner_rank = scored_0[:, first_rows, 0].astype(jnp.int32)
    send_second = jnp.sum(
        jnp.where(owner_rank[None, :] == ranks[:, None], ranks[None, :], 0), axis=1
    )
    tagged_0 = exchange(permute_in(send_second, scored_0, (0, first_rows + GROUP)))
    owned_0 = halves(tagged_0, first_rows)
    live = tagged_0[:, first_rows + GROUP // 2, 0].astype(jnp.int32)

    scored_here = scorer.reshape(dp_size, users) == dp_rank
    place = jnp.sum(
        jnp.where(scored_here, score_slot.reshape(dp_size, users), 0), axis=1
    ) - dp_rank * users
    own_scorer = lax.dynamic_slice_in_dim(scorer, dp_rank * users, users)
    order = jnp.sum(jnp.where(own_scorer[None, :] == ranks[:, None], local[None, :], 0), axis=1)
    scalars = jnp.concatenate([mp_rank[None], live]).astype(jnp.int32)

    lengths = jnp.take(history_length, order)
    position = jnp.arange(events, dtype=jnp.int32)
    distance = lengths[:, None] - position[None, :]
    inverse = 1.0 / (lengths + 1).astype(jnp.float32)
    spread = jnp.broadcast_to(inverse[:, None], (users, events))
    bias = 0.5 * bucket_bias(distance, time_bias)
    own_bias = jnp.broadcast_to(0.5 * time_bias[:, 0][:, None, None], bias.shape)
    info = [bias[h] for h in range(heads)] + [own_bias[h] for h in range(heads)]
    info = info + [jnp.where(distance > 0, spread, 0.0), spread]
    info = info + [jnp.zeros_like(spread)] * (-len(info) % 8)
    rows_info = jnp.stack(info, axis=1)

    def padded(count):
        return (jnp.maximum(count - first_rows, 0) + (GROUP - 1)) // GROUP * GROUP

    groups = padded(live)
    has = groups > 0
    earlier = local[None, :] < local[:, None]
    count = jnp.sum(has.astype(jnp.int32))
    seat = jnp.where(
        has,
        jnp.sum((earlier & has[None, :]).astype(jnp.int32), axis=1),
        count + jnp.sum((earlier & ~has[None, :]).astype(jnp.int32), axis=1),
    )
    seated = seat[None, :] == local[:, None]

    def by_seat(values):
        return jnp.sum(jnp.where(seated, values[None, :], 0), axis=1).astype(jnp.int32)

    seat_slots = by_seat(local)
    seat_order = by_seat(order)
    seat_scalars = jnp.concatenate([mp_rank[None], by_seat(live)]).astype(jnp.int32)
    seat_offsets = jnp.sum(
        jnp.where(seat[None, :] < local[:, None], groups[None, :], 0), axis=1
    ).astype(jnp.int32)
    seat_offsets = jnp.minimum(seat_offsets, SIZE)
    rank = mp_rank[None].astype(jnp.int32)
    seat_last = (jnp.maximum(count - 1, 0) // BATCH)[None].astype(jnp.int32)

    turned = (mp_rank + (mp_size - jnp.arange(mp_size, dtype=jnp.int32))) % mp_size
    weight_in = jnp.take(input_weight.reshape(mp_size, part, -1), turned, axis=0)
    weight_in = weight_in.reshape(input_weight.shape)

    def by_quarter(gated):
        return [gated[0]] + [shifted(gated[k], k) for k in range(1, mp_size)]

    rows_1 = permute_in(send_first, candidates, PIECES[1])
    rows_1, owned_0, rows_info, weight_in, *weights_out = lax.optimization_barrier(
        (rows_1, owned_0, rows_info, weight_in, *weights_out)
    )
    low_0, high_0 = owned_0
    full_low = [low_0, shifted(low_0, 1), None, shifted(low_0, 3)]
    full_low[2] = shifted(full_low[1], 1)
    full_high = [high_0, shifted(high_0, 1), None, shifted(high_0, 3)]
    full_high[2] = shifted(full_high[3], 3)
    owned_1 = exchange(permute_in(send_second, exchange(rows_1), (0, second_rows)))
    owned_1, groups = lax.optimization_barrier((owned_1, groups))
    packed = pack(seat_slots, seat_offsets, owned_1, SIZE)
    def attend_all(full):
        return attend(full, weight_in, history_cache, order, rank, rows_info, heads)

    full_1 = [[packed]] + [[shifted(packed, k)] for k in range(1, mp_size)]
    gated_0 = attend_all((full_low, full_high))
    gated_1 = attend_packed(
        full_1,
        weight_in,
        history_cache,
        seat_order,
        seat_offsets,
        seat_slots,
        seat_last,
        rank,
        rows_info,
        second_rows,
        heads,
    )
    done_0 = project_out(
        by_quarter(gated_0), (full_low, full_high), weights_out, scalars, 0
    )
    done = project_out_packed(
        by_quarter(gated_1),
        full_1,
        weights_out,
        seat_scalars,
        seat_slots,
        seat_offsets,
        1,
        done_0,
    )

    def unpacked(done, rows):
        every = [rows] + [shifted(rows, k) for k in range(1, mp_size)]
        both = [[r[: users // 2] for r in every], [r[users // 2 :] for r in every]]
        gated = by_quarter(attend_all(both))
        return project_out(gated, both, weights_out, scalars, 1, done)

    done = lax.cond(
        jnp.sum(groups) > SIZE, unpacked, lambda done, rows: done, done, owned_1
    )
    results = lax.all_to_all(
        done.reshape((-1,) + done.shape[2:]), ("dp", "mp"), split_axis=0, concat_axis=0, tiled=True
    )
    return permute_out(place, results.reshape(done.shape))


def solution(mesh):
    in_specs = (
        P("dp", None, "mp"),
        P("dp"),
        P("dp"),
        P(),
        P("dp", None, "mp"),
        P("dp"),
        P(None, "mp"),
        P("mp", None),
        P("mp", None),
    )
    out_specs = P("dp", None, "mp")
    return jax.shard_map(
        per_device, mesh=mesh, in_specs=in_specs, out_specs=out_specs, check_vma=False
    )
```

```python
import math

import jax
import jax.numpy as jnp
from jax import lax
from jax.experimental import pallas as pl
from jax.experimental.pallas import tpu as pltpu
from jax.sharding import PartitionSpec as P

HD = 128
EPSILON = 1e-05
VMEM = 48 * 1024 * 1024

PIECES = ((0, 64), (64, 64))
BATCH = 8
SIZE = 1088
GROUP = 16


def permute_out(index, results):
    users, mp, pieces, quarter, width = results.shape
    rows = pieces * mp * quarter

    def body(index_ref, src, out, buffer, sem):
        def store(i):
            return pltpu.make_async_copy(buffer.at[i], out.at[index_ref[i]], sem.at[i])

        for i in range(users):
            for n in range(pieces):
                for q in range(mp):
                    at = (n * mp + q) * quarter
                    buffer[i, at : at + quarter, :] = src[i, q, n]
            store(i).start()
        for i in range(users):
            store(i).wait()

    return pl.pallas_call(
        body,
        out_shape=jax.ShapeDtypeStruct((users, rows, width), results.dtype),
        in_specs=[
            pl.BlockSpec(memory_space=pltpu.SMEM),
            pl.BlockSpec(memory_space=pltpu.VMEM),
        ],
        out_specs=pl.BlockSpec(memory_space=pl.ANY),
        scratch_shapes=[
            pltpu.VMEM((users, rows, width), results.dtype),
            pltpu.SemaphoreType.DMA((users,)),
        ],
        compiler_params=pltpu.CompilerParams(vmem_limit_bytes=VMEM),
    )(index, results)


def permute_in(index, whole, piece, tags=()):
    users, _, width = whole.shape
    start, size = piece
    rows = size + GROUP if tags else size

    def body(index_ref, *refs):
        src, out = refs[-2:]
        upper = lax.broadcasted_iota(jnp.int32, (GROUP, width), 0) < GROUP // 2
        for i in range(users):
            at = index_ref[i]
            out[i, :size, :] = src[at, start : start + size, :]
            if tags:
                tag = jnp.where(upper, refs[0][at], refs[1][at])
                out[i, size:, :] = tag.astype(jnp.float32).astype(whole.dtype)

    return pl.pallas_call(
        body,
        out_shape=jax.ShapeDtypeStruct((users, rows, width), whole.dtype),
        in_specs=[pl.BlockSpec(memory_space=pltpu.SMEM)] * (1 + len(tags))
        + [pl.BlockSpec(memory_space=pltpu.VMEM)],
        out_specs=pl.BlockSpec(memory_space=pltpu.VMEM),
        compiler_params=pltpu.CompilerParams(vmem_limit_bytes=VMEM),
    )(index, *tags, whole)


def halves(rows, size):
    users, _, width = rows.shape
    half = users // 2

    def body(src, low, high, sem):
        copies = [
            pltpu.make_async_copy(
                src.at[pl.ds(n * half, half), pl.ds(0, size)], (low, high)[n], sem.at[n]
            )
            for n in range(2)
        ]
        for copy in copies:
            copy.start()
        for copy in copies:
            copy.wait()

    return pl.pallas_call(
        body,
        out_shape=[pltpu.HBM((half, size, width), rows.dtype)] * 2,
        in_specs=[pl.BlockSpec(memory_space=pltpu.VMEM)],
        out_specs=[pl.BlockSpec(memory_space=pltpu.HBM)] * 2,
        scratch_shapes=[pltpu.SemaphoreType.DMA((2,))],
        compiler_params=pltpu.CompilerParams(vmem_limit_bytes=VMEM),
    )(rows)


def attend_batch(projected, caches, infos, h, heads):
    inv_scale = 1.0 / math.sqrt(HD)
    batch = len(projected)
    rows = projected[0].shape[0]
    scores = [
        lax.dot_general(
            p[:, 2 * HD : 3 * HD],
            cache[0],
            (((1,), (1,)), ((), ())),
            preferred_element_type=jnp.float32,
        )
        for p, cache in zip(projected, caches)
    ]
    scores = [s * (0.5 * inv_scale) + info[h : h + 1, :] for s, info in zip(scores, infos)]
    weights = [
        ((s + s * jnp.tanh(s)) * info[2 * heads : 2 * heads + 1, :]).astype(jnp.bfloat16)
        for s, info in zip(scores, infos)
    ]
    summed = [
        jnp.dot(w, cache[1], preferred_element_type=jnp.float32)
        for w, cache in zip(weights, caches)
    ]
    whole = jnp.concatenate(projected, axis=0)
    gate, value, query, key = [
        whole[:, k * HD : (k + 1) * HD].astype(jnp.float32) for k in range(4)
    ]
    inverse = jnp.concatenate(
        [
            jnp.broadcast_to(info[2 * heads + 1 : 2 * heads + 2, :HD], (rows, HD))
            for info in infos
        ],
        axis=0,
    )
    own = jnp.sum(query * key, axis=-1, keepdims=True)
    own = own * (0.5 * inv_scale) + infos[0][heads + h : heads + h + 1, :HD]
    own = (own + own * jnp.tanh(own)) * inverse
    own = own.astype(jnp.bfloat16).astype(jnp.float32)
    combined = jnp.concatenate(summed, axis=0) + own * value
    head_mean = jnp.mean(combined, axis=-1, keepdims=True)
    centred = combined - head_mean
    head_var = jnp.mean(centred * centred, axis=-1, keepdims=True)
    return (centred * lax.rsqrt(head_var + EPSILON) * gate).astype(jnp.bfloat16)


def spread_quarters(whole_ref, out_refs, rows, rank):
    mp = len(out_refs)
    quarter = rows // mp
    for k in range(mp):
        at = ((rank + k) % mp) * quarter
        for b in range(BATCH):
            out_refs[k][b] = whole_ref[pl.ds(pl.multiple_of(b * rows + at, GROUP), quarter), :]


def normalise(parts):
    parts = [p.astype(jnp.float32) for p in parts]
    width = len(parts) * parts[0].shape[1]
    mean = sum(jnp.sum(p, axis=-1, keepdims=True) for p in parts) * (1.0 / width)
    parts = [p - mean for p in parts]
    var = sum(jnp.sum(p * p, axis=-1, keepdims=True) for p in parts) * (1.0 / width)
    factor = lax.rsqrt(var + EPSILON)
    return jnp.concatenate([(p * factor).astype(jnp.bfloat16) for p in parts], axis=1)


def silu_dot(normed, weight):
    half = 0.5 * jnp.dot(normed, weight, preferred_element_type=jnp.float32)
    return (half + half * jnp.tanh(half)).astype(jnp.bfloat16)


def head_cache(hist_ref, h):
    return (
        hist_ref[0, :, 2 * h * HD : (2 * h + 1) * HD],
        hist_ref[0, :, (2 * h + 1) * HD : (2 * h + 2) * HD],
    )


def attend(full, weight, history, order, rank, rows_info, heads):
    mp = len(full[0])
    half, rows, part = full[0][0].shape
    users = order.shape[0]
    events, kv_width = history.shape[1:]
    quarter = rows // mp
    total = BATCH * rows
    width = heads * HD
    per_half = half // BATCH

    def body(order_ref, rank_ref, *refs):
        full_refs, weight_ref, info_ref = refs[: 2 * mp], refs[2 * mp], refs[2 * mp + 1]
        hist_refs = refs[2 * mp + 2 : 2 * mp + 2 + BATCH]
        out_refs, store = refs[-1 - mp : -1], refs[-1]
        low = pl.program_id(0) < per_half
        parts = [jnp.where(low, full_refs[k][...], full_refs[mp + k][...]) for k in range(mp)]
        normed = normalise([p.reshape(total, part) for p in parts])
        infos = [info_ref.at[b] for b in range(BATCH)]
        for h in range(heads):
            projected = silu_dot(normed, weight_ref[:, h * 4 * HD : (h + 1) * 4 * HD])
            store[:, h * HD : (h + 1) * HD] = attend_batch(
                [projected[b * rows : (b + 1) * rows] for b in range(BATCH)],
                [head_cache(hist_refs[b], h) for b in range(BATCH)],
                infos,
                h,
                heads,
            )
        spread_quarters(store, out_refs, rows, rank_ref[0])

    def full_spec(n):
        return pl.BlockSpec(
            (BATCH, rows, part), lambda i, *_: (jnp.clip(i - n * per_half, 0, per_half - 1), 0, 0)
        )

    def hist_spec(b):
        return pl.BlockSpec((1, events, kv_width), lambda i, order, _: (order[i * BATCH + b], 0, 0))

    return pl.pallas_call(
        body,
        out_shape=[pltpu.HBM((users, quarter, width), jnp.bfloat16)] * mp,
        grid_spec=pltpu.PrefetchScalarGridSpec(
            num_scalar_prefetch=2,
            grid=(users // BATCH,),
            in_specs=[full_spec(n) for n in range(2) for _ in range(mp)]
            + [
                pl.BlockSpec(weight.shape, lambda i, *_: (0, 0)),
                pl.BlockSpec((BATCH,) + rows_info.shape[1:], lambda i, *_: (i, 0, 0)),
            ]
            + [hist_spec(b) for b in range(BATCH)],
            out_specs=[pl.BlockSpec((BATCH, quarter, width), lambda i, *_: (i, 0, 0))] * mp,
            scratch_shapes=[pltpu.VMEM((total, width), jnp.bfloat16)],
        ),
        compiler_params=pltpu.CompilerParams(vmem_limit_bytes=VMEM),
    )(order, rank, *full[0], *full[1], weight, rows_info, *([history] * BATCH))


def pack(slots, offsets, rows, size):
    users, count, width = rows.shape

    def body(slots_ref, offsets_ref, rows_ref, out, buffer, sem):
        for j in range(users):
            at = pl.multiple_of(offsets_ref[j], GROUP)
            buffer[pl.ds(at, count), :] = rows_ref[slots_ref[j]]
        copy = pltpu.make_async_copy(buffer.at[pl.ds(0, size)], out, sem)
        copy.start()
        copy.wait()

    return pl.pallas_call(
        body,
        out_shape=pltpu.HBM((size, width), rows.dtype),
        in_specs=[
            pl.BlockSpec(memory_space=pltpu.SMEM),
            pl.BlockSpec(memory_space=pltpu.SMEM),
            pl.BlockSpec(memory_space=pltpu.VMEM),
        ],
        out_specs=pl.BlockSpec(memory_space=pltpu.HBM),
        scratch_shapes=[
            pltpu.VMEM((size + count, width), rows.dtype),
            pltpu.SemaphoreType.DMA,
        ],
        compiler_params=pltpu.CompilerParams(vmem_limit_bytes=VMEM),
    )(slots, offsets, rows)


def attend_packed(
    full, weight, history, order, offsets, seats, last, rank, rows_info, rows, heads
):
    mp = len(full)
    part = full[0][0].shape[1]
    size = sum(array.shape[0] for array in full[0])
    users = order.shape[0]
    events, kv_width = history.shape[1:]
    quarter = rows // mp
    blocks = 2
    block = size // blocks
    count = sum(len(arrays) for arrays in full)

    def body(
        order_ref, offsets_ref, seats_ref, last_ref, rank_ref, *refs
    ):
        weight_ref, info_ref = refs[count], refs[count + 1]
        hist_refs = refs[count + 2 : count + 2 + BATCH]
        out_refs = refs[count + 2 + BATCH : count + 2 + BATCH + mp]
        store, merged = refs[-2:]
        step = pl.program_id(0)

        @pl.when(step < blocks)
        def _():
            parts, at = [], 0
            for arrays in full:
                block_rows = refs[at][...]
                if len(arrays) > 1:
                    low = step < arrays[0].shape[0] // block
                    block_rows = jnp.where(low, block_rows, refs[at + 1][...])
                parts.append(block_rows)
                at = at + len(arrays)
            normed = normalise(parts)
            at = pl.multiple_of(step * block, GROUP)
            store[pl.ds(at, block), :] = silu_dot(normed, weight_ref[...])

        @pl.when((step >= blocks) & (step - blocks <= last_ref[0]))
        def _():
            seats = [(step - blocks) * BATCH + b for b in range(BATCH)]
            starts = [pl.multiple_of(offsets_ref[j], GROUP) for j in seats]
            infos = [info_ref.at[seats_ref[j]] for j in seats]
            for h in range(heads):
                merged[:, h * HD : (h + 1) * HD] = attend_batch(
                    [store[pl.ds(at, rows), h * 4 * HD : (h + 1) * 4 * HD] for at in starts],
                    [head_cache(hist_refs[b], h) for b in range(BATCH)],
                    infos,
                    h,
                    heads,
                )
            spread_quarters(merged, out_refs, rows, rank_ref[0])

    def full_spec(array, n):
        steps = array.shape[0] // block
        return pl.BlockSpec((block, part), lambda i, *_: (jnp.clip(i - n * steps, 0, steps - 1), 0))

    def batch_of(i):
        return jnp.maximum(i - blocks, 0)

    def hist_spec(b):
        return pl.BlockSpec(
            (1, events, kv_width),
            lambda i, order, offsets, seats, last, rank: (
                order[jnp.minimum(batch_of(i), last[0]) * BATCH + b],
                0,
                0,
            ),
        )

    width = heads * HD
    return pl.pallas_call(
        body,
        out_shape=[pltpu.HBM((users, quarter, width), jnp.bfloat16)] * mp,
        grid_spec=pltpu.PrefetchScalarGridSpec(
            num_scalar_prefetch=5,
            grid=(blocks + users // BATCH,),
            in_specs=[full_spec(array, n) for arrays in full for n, array in enumerate(arrays)]
            + [
                pl.BlockSpec(weight.shape, lambda i, *_: (0, 0)),
                pl.BlockSpec(rows_info.shape, lambda i, *_: (0, 0, 0)),
            ]
            + [hist_spec(b) for b in range(BATCH)],
            out_specs=[pl.BlockSpec((BATCH, quarter, width), lambda i, *_: (batch_of(i), 0, 0))]
            * mp,
            scratch_shapes=[
                pltpu.VMEM((size + rows, weight.shape[1]), jnp.bfloat16),
                pltpu.VMEM((BATCH * rows, width), jnp.bfloat16),
            ],
        ),
        compiler_params=pltpu.CompilerParams(vmem_limit_bytes=VMEM),
    )(order, offsets, seats, last, rank, *sum(full, []), weight, rows_info, *([history] * BATCH))


def rank_dot(gated, weights):
    terms = [
        jnp.dot(g, w, preferred_element_type=jnp.float32) for g, w in zip(gated, weights)
    ]
    return sum(terms[1:], terms[0])


def project_out(gated, full, weights, scalars, piece, before=None):
    mp = len(gated)
    users, quarter, part = gated[0].shape
    out_part = weights[0].shape[1] // mp
    batch = 8
    per_half = users // 2 // batch
    start = PIECES[piece][0]
    extra = () if before is None else (before,)

    def body(scalar_ref, *refs):
        full_refs, gated_refs = refs[: 2 * mp], refs[2 * mp : 3 * mp]
        weight_refs, out_ref = refs[3 * mp : 4 * mp], refs[-1]
        step = pl.program_id(0)
        rank = scalar_ref[0]
        rows = [g[...].reshape(batch * quarter, part) for g in gated_refs]
        row = lax.broadcasted_iota(jnp.int32, (quarter, out_part), 0) + (start + rank * quarter)
        for k in range(mp):
            column = (rank + (mp - k)) % mp
            at = pl.multiple_of(column * out_part, out_part)
            acc = rank_dot(rows, [w[:, pl.ds(at, out_part)] for w in weight_refs])
            for b in range(batch):
                alive = row < scalar_ref[1 + step * batch + b]
                residual = jnp.where(step < per_half, full_refs[k][b], full_refs[mp + k][b])
                mine = acc[b * quarter : (b + 1) * quarter] + residual.astype(jnp.float32)
                out_ref[b, column, 0] = jnp.where(alive, mine, 0.0).astype(jnp.bfloat16)

    def full_spec(n):
        return pl.BlockSpec(
            (batch, quarter, part),
            lambda i, s: (jnp.clip(i - n * per_half, 0, per_half - 1), s[0], 0),
        )

    return pl.pallas_call(
        body,
        out_shape=jax.ShapeDtypeStruct((users, mp, len(PIECES), quarter, out_part), jnp.bfloat16),
        grid_spec=pltpu.PrefetchScalarGridSpec(
            num_scalar_prefetch=1,
            grid=(users // batch,),
            in_specs=[full_spec(n) for n in range(2) for _ in range(mp)]
            + [pl.BlockSpec((batch, quarter, part), lambda i, s: (i, 0, 0)) for _ in gated]
            + [pl.BlockSpec(w.shape, lambda i, s: (0, 0)) for w in weights]
            + [pl.BlockSpec(memory_space=pl.ANY) for _ in extra],
            out_specs=pl.BlockSpec(
                (batch, mp, 1, quarter, out_part), lambda i, s: (i, 0, piece, 0, 0)
            ),
        ),
        input_output_aliases={1 + 4 * mp: 0} if extra else {},
        compiler_params=pltpu.CompilerParams(vmem_limit_bytes=VMEM),
    )(scalars, *full[0], *full[1], *gated, *weights, *extra)


def project_out_packed(gated, full, weights, scalars, slots, offsets, piece, before):
    mp = len(gated)
    users, quarter, part = gated[0].shape
    size = full[0][0].shape[0]
    out_part = weights[0].shape[1] // mp
    start = PIECES[piece][0]

    def body(scalar_ref, slots_ref, offsets_ref, *refs):
        full_refs, gated_refs = refs[:mp], refs[mp : 2 * mp]
        weight_refs = refs[2 * mp : 3 * mp]
        out_ref, store, sem = refs[-3:]
        rank = scalar_ref[0]
        rows = [g[...].reshape(users * quarter, part) for g in gated_refs]
        row = lax.broadcasted_iota(jnp.int32, (quarter, out_part), 0) + (start + rank * quarter)

        def copy(k):
            column = (rank + (mp - k)) % mp
            return pltpu.make_async_copy(store.at[k], out_ref.at[:, column, piece], sem.at[k])

        for k in range(mp):
            column = (rank + (mp - k)) % mp
            first = pl.multiple_of(column * out_part, out_part)
            acc = rank_dot(rows, [w[:, pl.ds(first, out_part)] for w in weight_refs])
            for j in range(users):
                at = jnp.minimum(offsets_ref[j] + rank * quarter, size - quarter)
                residual = full_refs[k][pl.ds(pl.multiple_of(at, GROUP), quarter), :]
                mine = acc[j * quarter : (j + 1) * quarter] + residual.astype(jnp.float32)
                alive = row < scalar_ref[1 + j]
                store[k, slots_ref[j]] = jnp.where(alive, mine, 0.0).astype(jnp.bfloat16)
            copy(k).start()
        for k in range(mp):
            copy(k).wait()

    arrays = [array for arrays in full for array in arrays]
    return pl.pallas_call(
        body,
        out_shape=jax.ShapeDtypeStruct((users, mp, len(PIECES), quarter, out_part), jnp.bfloat16),
        in_specs=[pl.BlockSpec(memory_space=pltpu.SMEM)] * 3
        + [pl.BlockSpec(memory_space=pltpu.VMEM)] * (3 * mp)
        + [pl.BlockSpec(memory_space=pl.ANY)],
        out_specs=pl.BlockSpec(memory_space=pl.ANY),
        scratch_shapes=[
            pltpu.VMEM((mp, users, quarter, out_part), jnp.bfloat16),
            pltpu.SemaphoreType.DMA((mp,)),
        ],
        input_output_aliases={3 + 3 * mp: 0},
        compiler_params=pltpu.CompilerParams(vmem_limit_bytes=VMEM),
    )(scalars, slots, offsets, *arrays, *gated, *weights, before)


def bucket_bias(distance, time_bias):
    bias = jnp.broadcast_to(time_bias[:, 0][:, None, None], time_bias.shape[:1] + distance.shape)
    for k in range(time_bias.shape[1] - 1):
        bias = jnp.where((distance >= 2**k)[None], time_bias[:, k + 1][:, None, None], bias)
    return bias


def per_device(
    candidates,
    live_counts,
    request_user,
    score_slot,
    history_cache,
    history_length,
    input_weight,
    time_bias,
    output_weight,
):
    dp_size = lax.axis_size("dp")
    dp_rank = lax.axis_index("dp")
    mp_rank = lax.axis_index("mp")
    users, slots, part = candidates.shape
    events = history_cache.shape[1]
    heads = time_bias.shape[0]
    ranks = jnp.arange(dp_size, dtype=jnp.int32)
    local = jnp.arange(users, dtype=jnp.int32)
    scorer = score_slot // users

    target = jnp.take(scorer, request_user)
    send_first = jnp.sum(jnp.where(target[None, :] == ranks[:, None], local[None, :], 0), axis=1)
    def exchange(rows):
        return lax.all_to_all(rows, "dp", split_axis=0, concat_axis=0, tiled=True)

    mp_size = lax.axis_size("mp")

    def shifted(array, k):
        return lax.ppermute(array, "mp", [(i, (i + k) % mp_size) for i in range(mp_size)])

    first_rows, second_rows = PIECES[0][1], PIECES[1][1]
    weights_out = [output_weight] + [shifted(output_weight, k) for k in range(1, mp_size)]
    rows_0 = permute_in(send_first, candidates, PIECES[0], (request_user // users, live_counts))
    scored_0 = exchange(rows_0)
    owner_rank = scored_0[:, first_rows, 0].astype(jnp.int32)
    send_second = jnp.sum(
        jnp.where(owner_rank[None, :] == ranks[:, None], ranks[None, :], 0), axis=1
    )
    tagged_0 = exchange(permute_in(send_second, scored_0, (0, first_rows + GROUP)))
    owned_0 = halves(tagged_0, first_rows)
    live = tagged_0[:, first_rows + GROUP // 2, 0].astype(jnp.int32)

    scored_here = scorer.reshape(dp_size, users) == dp_rank
    place = jnp.sum(
        jnp.where(scored_here, score_slot.reshape(dp_size, users), 0), axis=1
    ) - dp_rank * users
    own_scorer = lax.dynamic_slice_in_dim(scorer, dp_rank * users, users)
    order = jnp.sum(jnp.where(own_scorer[None, :] == ranks[:, None], local[None, :], 0), axis=1)
    scalars = jnp.concatenate([mp_rank[None], live]).astype(jnp.int32)

    lengths = jnp.take(history_length, order)
    position = jnp.arange(events, dtype=jnp.int32)
    distance = lengths[:, None] - position[None, :]
    inverse = 1.0 / (lengths + 1).astype(jnp.float32)
    spread = jnp.broadcast_to(inverse[:, None], (users, events))
    bias = 0.5 * bucket_bias(distance, time_bias)
    own_bias = jnp.broadcast_to(0.5 * time_bias[:, 0][:, None, None], bias.shape)
    info = [bias[h] for h in range(heads)] + [own_bias[h] for h in range(heads)]
    info = info + [jnp.where(distance > 0, spread, 0.0), spread]
    info = info + [jnp.zeros_like(spread)] * (-len(info) % 8)
    rows_info = jnp.stack(info, axis=1)

    def padded(count):
        return (jnp.maximum(count - first_rows, 0) + (GROUP - 1)) // GROUP * GROUP

    groups = padded(live)
    has = groups > 0
    earlier = local[None, :] < local[:, None]
    count = jnp.sum(has.astype(jnp.int32))
    seat = jnp.where(
        has,
        jnp.sum((earlier & has[None, :]).astype(jnp.int32), axis=1),
        count + jnp.sum((earlier & ~has[None, :]).astype(jnp.int32), axis=1),
    )
    seated = seat[None, :] == local[:, None]

    def by_seat(values):
        return jnp.sum(jnp.where(seated, values[None, :], 0), axis=1).astype(jnp.int32)

    seat_slots = by_seat(local)
    seat_order = by_seat(order)
    seat_scalars = jnp.concatenate([mp_rank[None], by_seat(live)]).astype(jnp.int32)
    seat_offsets = jnp.sum(
        jnp.where(seat[None, :] < local[:, None], groups[None, :], 0), axis=1
    ).astype(jnp.int32)
    seat_offsets = jnp.minimum(seat_offsets, SIZE)
    rank = mp_rank[None].astype(jnp.int32)
    seat_last = (jnp.maximum(count - 1, 0) // BATCH)[None].astype(jnp.int32)

    turned = (mp_rank + (mp_size - jnp.arange(mp_size, dtype=jnp.int32))) % mp_size
    weight_in = jnp.take(input_weight.reshape(mp_size, part, -1), turned, axis=0)
    weight_in = weight_in.reshape(input_weight.shape)

    def by_quarter(gated):
        return [gated[0]] + [shifted(gated[k], k) for k in range(1, mp_size)]

    rows_1 = permute_in(send_first, candidates, PIECES[1])
    rows_1, owned_0, rows_info, weight_in, *weights_out = lax.optimization_barrier(
        (rows_1, owned_0, rows_info, weight_in, *weights_out)
    )
    low_0, high_0 = owned_0
    full_low = [low_0, shifted(low_0, 1), None, shifted(low_0, 3)]
    full_low[2] = shifted(full_low[1], 1)
    full_high = [high_0, shifted(high_0, 1), None, shifted(high_0, 3)]
    full_high[2] = shifted(full_high[3], 3)
    owned_1 = exchange(permute_in(send_second, exchange(rows_1), (0, second_rows)))
    owned_1, groups = lax.optimization_barrier((owned_1, groups))
    packed = pack(seat_slots, seat_offsets, owned_1, SIZE)
    def attend_all(full):
        return attend(full, weight_in, history_cache, order, rank, rows_info, heads)

    full_1 = [[packed]] + [[shifted(packed, k)] for k in range(1, mp_size)]
    gated_0 = attend_all((full_low, full_high))
    gated_1 = attend_packed(
        full_1,
        weight_in,
        history_cache,
        seat_order,
        seat_offsets,
        seat_slots,
        seat_last,
        rank,
        rows_info,
        second_rows,
        heads,
    )
    done_0 = project_out(
        by_quarter(gated_0), (full_low, full_high), weights_out, scalars, 0
    )
    done = project_out_packed(
        by_quarter(gated_1),
        full_1,
        weights_out,
        seat_scalars,
        seat_slots,
        seat_offsets,
        1,
        done_0,
    )

    def unpacked(done, rows):
        every = [rows] + [shifted(rows, k) for k in range(1, mp_size)]
        both = [[r[: users // 2] for r in every], [r[users // 2 :] for r in every]]
        gated = by_quarter(attend_all(both))
        return project_out(gated, both, weights_out, scalars, 1, done)

    done = lax.cond(
        jnp.sum(groups) > SIZE, unpacked, lambda done, rows: done, done, owned_1
    )
    results = lax.all_to_all(
        done.reshape((-1,) + done.shape[2:]), ("dp", "mp"), split_axis=0, concat_axis=0, tiled=True
    )
    return permute_out(place, results.reshape(done.shape))


def solution(mesh):
    in_specs = (
        P("dp", None, "mp"),
        P("dp"),
        P("dp"),
        P(),
        P("dp", None, "mp"),
        P("dp"),
        P(None, "mp"),
        P("mp", None),
        P("mp", None),
    )
    out_specs = P("dp", None, "mp")
    return jax.shard_map(
        per_device, mesh=mesh, in_specs=in_specs, out_specs=out_specs, check_vma=False
    )
```
